128 devices in a mesh: dap: 8 (over y_hi, z), bulk: 16 (over y_lo, x, core).
Axes of the slice: x: 4, y: 4 (y_hi: 2, y_lo: 2; y = y_hi * 2 + y_lo), z: 4, core: 2. Of those that a mesh axis runs over, the one named last changes fastest.
Arguments:
- stacked_relatives_tensor: bfloat16 [128, 1024, 256], P('bulk', 'dap'), may hold values from -6 to 6
- couple_embedding: bfloat16 [1024, 1024, 128], P(('dap', 'bulk')), may hold values from -6 to 6
- relatives_rescaler: float32 [256], replicated, may hold values from 0.25 to 2
- averaged_lhs_weights: bfloat16 [256, 32], replicated, may hold values from -0.375 to 0.375
- averaged_rhs_weights: bfloat16 [256, 32], replicated, may hold values from -0.375 to 0.375
- mean_final_linear: bfloat16 [1024, 128], replicated, may hold values from -0.75 to 0.75
- couple_scale_vector: float32 [128], replicated, may hold values from 0.25 to 2
- first_linear_map: bfloat16 [128, 128], replicated, may hold values from -0.5 to 0.5
- first_sigmoid_factor: bfloat16 [128, 128], replicated, may hold values from -0.5 to 0.5
- second_linear_map: bfloat16 [128, 128], replicated, may hold values from -0.5 to 0.5
- second_sigmoid_factor: bfloat16 [128, 128], replicated, may hold values from -0.5 to 0.5
- final_sigmoid_factor: bfloat16 [128, 128], replicated, may hold values from -0.5 to 0.5
- trio_scale_vector: float32 [128], replicated, may hold values from 0.25 to 2
- trio_final_linear: bfloat16 [128, 128], replicated, may hold values from -0.5 to 0.5
Outputs:
- new_pair: bfloat16 [1024, 1024, 128], P(('dap', 'bulk'))
The draws below stay inside these ranges and needn't reach their ends.
All inputs are finite; a program needn't handle non-finite values.
Results may differ from the reference program's by a relative error of at most 0.012.
Values may be sent and summed in bfloat16 or wider, within the bound.
No kernel may reach another device: no remote copies, remote signals or barrier semaphores. Data moves between devices by JAX's collectives and lax.ppermute only.
A program may use at most 192 MiB of HBM per device.

```python
import math
import jax
import jax.numpy as jnp
from jax import lax

STACK_WIDTH = 256
CZ = 128
INNER_WIDTH = 32
CT = 128
SEARCH_DEPTH = 128
PEPTIDE_LENGTH = 1024


def levels(own_key, dims, cuts, smallest, high):
    factor_of = 1.0
    for position, shards_of in cuts:
        draws = jax.random.uniform(jax.random.fold_in(jax.random.fold_in(own_key, 6), position), (shards_of,), jnp.float32, smallest / len(cuts), high / len(cuts))
        factor_of = factor_of * jnp.repeat(jnp.exp(draws), dims[position] // shards_of).reshape((-1,) + (1,) * (len(dims) - 1 - position))
    return factor_of


def scatter_about(key, extent, deviation, limit, cuts=(), dtype=jnp.bfloat16):
    values = jax.random.normal(key, extent, jnp.float32) * deviation
    if len(cuts) > 0:
        values = levels(key, extent, cuts, -0.22, 0.18) * values
    return jnp.clip(values, min=-limit, max=limit).astype(dtype)


def setup_inputs(seed: int = 0) -> dict:
    splits = jax.random.split(jax.random.key(seed), 15)
    return {
        "stacked_relatives_tensor": scatter_about(splits[0], (SEARCH_DEPTH, PEPTIDE_LENGTH, STACK_WIDTH), 1.0, 6.0, ((0, 16), (1, 8))),
        "couple_embedding": scatter_about(splits[1], (PEPTIDE_LENGTH, PEPTIDE_LENGTH, CZ), 1.0, 6.0, ((0, 128),)),
        "relatives_rescaler": jnp.clip(jax.random.uniform(splits[2], (STACK_WIDTH,), jnp.float32, 0.25, 2.0), 0.25, 2.0),
        "averaged_lhs_weights": scatter_about(splits[3], (STACK_WIDTH, INNER_WIDTH), STACK_WIDTH ** -0.5, 0.375),
        "averaged_rhs_weights": scatter_about(splits[4], (STACK_WIDTH, INNER_WIDTH), STACK_WIDTH ** -0.5, 0.375),
        "mean_final_linear": scatter_about(splits[5], (INNER_WIDTH * INNER_WIDTH, CZ), 64 ** -0.5, 0.75),
        "couple_scale_vector": jnp.clip(jax.random.uniform(splits[6], (CZ,), jnp.float32, 0.25, 2.0), 0.25, 2.0),
        "first_linear_map": scatter_about(splits[7], (CZ, CT), CZ ** -0.5, 0.5),
        "first_sigmoid_factor": scatter_about(splits[8], (CZ, CT), CZ ** -0.5, 0.5),
        "second_linear_map": scatter_about(splits[9], (CZ, CT), CZ ** -0.5, 0.5),
        "second_sigmoid_factor": scatter_about(splits[10], (CZ, CT), CZ ** -0.5, 0.5),
        "final_sigmoid_factor": scatter_about(splits[11], (CZ, CZ), CZ ** -0.5, 0.5),
        "trio_scale_vector": jnp.clip(jax.random.uniform(splits[12], (CT,), jnp.float32, 0.25, 2.0), 0.25, 2.0),
        "trio_final_linear": scatter_about(splits[13], (CT, CZ), CT ** -0.5, 0.5),
    }


def standardize_features(values, gain):
    center = values - lax.optimization_barrier(jnp.mean(values, axis=-1, keepdims=True))
    spread = lax.optimization_barrier(jnp.mean(center * center, axis=-1, keepdims=True))
    return center / jnp.sqrt(spread + 1e-05) * gain

def reference(stacked_relatives_tensor, couple_embedding, relatives_rescaler, averaged_lhs_weights, averaged_rhs_weights, mean_final_linear, couple_scale_vector, first_linear_map, first_sigmoid_factor, second_linear_map, second_sigmoid_factor, final_sigmoid_factor, trio_scale_vector, trio_final_linear):
    homolog_standardized = standardize_features(stacked_relatives_tensor.astype(jnp.float32), relatives_rescaler).astype(jnp.bfloat16)
    left_alignment_projection = jnp.dot(homolog_standardized, averaged_lhs_weights, preferred_element_type=jnp.float32).astype(jnp.bfloat16)
    right_alignment_projection = jnp.dot(homolog_standardized, averaged_rhs_weights, preferred_element_type=jnp.float32).astype(jnp.bfloat16)
    row_block_count = math.gcd(PEPTIDE_LENGTH, 64)
    right_flattened_rows = right_alignment_projection.reshape(SEARCH_DEPTH, PEPTIDE_LENGTH * INNER_WIDTH)

    def opm_rows(left_block):
        left_flattened_rows = left_block.transpose(1, 2, 0).reshape(row_block_count * INNER_WIDTH, SEARCH_DEPTH)
        triangle_products = jnp.dot(left_flattened_rows, right_flattened_rows, preferred_element_type=jnp.float32) * (1.0 / SEARCH_DEPTH)
        triangle_products = triangle_products.astype(jnp.bfloat16).reshape(row_block_count, INNER_WIDTH, PEPTIDE_LENGTH, INNER_WIDTH)
        triangle_products = triangle_products.transpose(0, 2, 1, 3).reshape(row_block_count, PEPTIDE_LENGTH, INNER_WIDTH * INNER_WIDTH)
        return jnp.dot(triangle_products, mean_final_linear, preferred_element_type=jnp.float32)
    left_row_blocks = left_alignment_projection.reshape(SEARCH_DEPTH, PEPTIDE_LENGTH // row_block_count, row_block_count, INNER_WIDTH).transpose(1, 0, 2, 3)
    opm = lax.map(opm_rows, left_row_blocks).reshape(PEPTIDE_LENGTH, PEPTIDE_LENGTH, CZ)
    updated = (couple_embedding.astype(jnp.float32) + opm).astype(jnp.bfloat16)
    pair_normed = standardize_features(updated.astype(jnp.float32), couple_scale_vector).astype(jnp.bfloat16)
    left_tri = (jax.nn.sigmoid(jnp.dot(pair_normed, first_sigmoid_factor, preferred_element_type=jnp.float32)) * jnp.dot(pair_normed, first_linear_map, preferred_element_type=jnp.float32)).astype(jnp.bfloat16)
    right_tri = (jax.nn.sigmoid(jnp.dot(pair_normed, second_sigmoid_factor, preferred_element_type=jnp.float32)) * jnp.dot(pair_normed, second_linear_map, preferred_element_type=jnp.float32)).astype(jnp.bfloat16)
    gate = jax.nn.sigmoid(jnp.dot(pair_normed, final_sigmoid_factor, preferred_element_type=jnp.float32))
    left_chan = left_tri.transpose(2, 0, 1).reshape(CT // 8, 8, PEPTIDE_LENGTH, PEPTIDE_LENGTH)
    right_chan = right_tri.transpose(2, 0, 1).reshape(CT // 8, 8, PEPTIDE_LENGTH, PEPTIDE_LENGTH)

    def tri_block(operands):
        left_part, right_part = operands
        return jnp.einsum('cik,cjk->cij', left_part.astype(jnp.float32), right_part.astype(jnp.float32), precision=lax.Precision.HIGHEST).astype(jnp.bfloat16)
    mixed = lax.map(tri_block, (left_chan, right_chan)).reshape(CT, PEPTIDE_LENGTH, PEPTIDE_LENGTH)
    mixed_rows = mixed.transpose(1, 2, 0).astype(jnp.float32)
    mixed_normed = standardize_features(mixed_rows, trio_scale_vector).astype(jnp.bfloat16)
    output_term = jnp.dot(mixed_normed, trio_final_linear, preferred_element_type=jnp.float32)
    return (updated.astype(jnp.float32) + gate * output_term).astype(jnp.bfloat16)
```

```python
import jax
import jax.numpy as jnp
from jax import lax
from jax.experimental import pallas as pl
from jax.experimental.pallas import tpu as pltpu
from jax.sharding import Mesh, PartitionSpec as P

ALL = ("dap", "chip", "core")


def standardize_features(values, gain, axis=-1):
    center = values - jnp.mean(values, axis=axis, keepdims=True)
    spread = jnp.mean(center * center, axis=axis, keepdims=True)
    return center / jnp.sqrt(spread + 1e-05) * gain


def opm_kernel(depth, right_ref, left_ref, weight_ref, out_ref, right_rows, mixer):
    groups, chips, _, width = right_ref.shape
    hidden = left_ref.shape[1]
    cols = right_rows.shape[0] // groups
    seqs = width // hidden
    channels = weight_ref.shape[1] // hidden

    @pl.when(pl.program_id(0) == 0)
    def _():
        for chip in range(chips):
            for group in range(groups):
                right_rows[group * cols : (group + 1) * cols, chip * width : (chip + 1) * width] = (
                    right_ref[group, chip, :cols, :]
                )

    expanded = jnp.dot(left_ref[...], weight_ref[...], preferred_element_type=jnp.float32) * (
        1.0 / depth
    )
    pair = left_ref.shape[0] // (chips * seqs)
    step = 16 // seqs
    for row in range(pair):
        for chip in range(chips):
            start = (row * chips + chip) * seqs
            for d in range(0, hidden, step):
                tile = jnp.concatenate(
                    [
                        expanded[start : start + seqs, k * channels : (k + 1) * channels]
                        for k in range(d, d + step)
                    ],
                    axis=0,
                )
                mixer[
                    chip * width + d * seqs : chip * width + (d + step) * seqs,
                    row * channels : (row + 1) * channels,
                ] = tile.astype(jnp.bfloat16)
    out = jnp.dot(right_rows[...], mixer[...], preferred_element_type=jnp.float32)
    for row in range(pair):
        out_ref[row] = out[:, row * channels : (row + 1) * channels].astype(out_ref.dtype)


def opm_rows(right, left, weight, depth, cols, dtype):
    groups, chips, rows_sent, width = right.shape
    rows, _, seqs, hidden = left.shape
    channels = weight.shape[1] // hidden
    flat = left.reshape(rows * chips * seqs, hidden)
    pair = 2
    return pl.pallas_call(
        lambda *refs: opm_kernel(depth, *refs),
        grid=(rows // pair,),
        in_specs=[
            pl.BlockSpec(right.shape, lambda i: (0, 0, 0, 0)),
            pl.BlockSpec((pair * chips * seqs, hidden), lambda i: (i, 0)),
            pl.BlockSpec(weight.shape, lambda i: (0, 0)),
        ],
        out_specs=pl.BlockSpec((pair, groups * cols, channels), lambda i: (i, 0, 0)),
        out_shape=jax.ShapeDtypeStruct((rows, groups * cols, channels), dtype),
        scratch_shapes=[
            pltpu.VMEM((groups * cols, chips * width), jnp.bfloat16),
            pltpu.VMEM((chips * width, pair * channels), jnp.bfloat16),
        ],
        compiler_params=pltpu.CompilerParams(vmem_limit_bytes=40 * 1024 * 1024),
        cost_estimate=pl.CostEstimate(
            flops=2 * rows * groups * cols * chips * width * channels,
            bytes_accessed=right.size * 2 + rows * groups * cols * channels * 4,
            transcendentals=0,
        ),
    )(right, flat, weight)


def gated_operand(pair_normed, proj_weight, gate_weight):
    linear_part = jnp.dot(pair_normed, proj_weight, preferred_element_type=jnp.float32)
    gate_part = jax.nn.sigmoid(
        jnp.dot(pair_normed, gate_weight, preferred_element_type=jnp.float32)
    )
    return (gate_part * linear_part).astype(jnp.bfloat16)


def body(
    stacked_relatives_tensor,
    couple_embedding,
    relatives_rescaler,
    averaged_lhs_weights,
    averaged_rhs_weights,
    mean_final_linear,
    couple_scale_vector,
    first_linear_map,
    first_sigmoid_factor,
    second_linear_map,
    second_sigmoid_factor,
    final_sigmoid_factor,
    trio_scale_vector,
    trio_final_linear,
):
    groups, chips, cores = (lax.axis_size(name) for name in ALL)
    devices = groups * chips * cores
    seqs, cols, features = stacked_relatives_tensor.shape
    hidden = averaged_lhs_weights.shape[1]
    depth = seqs * chips * cores
    rows, length, pair_width = couple_embedding.shape
    core = lax.axis_index("core")

    msa_normed = standardize_features(
        stacked_relatives_tensor.astype(jnp.float32), relatives_rescaler
    ).astype(jnp.bfloat16)
    left_msa = jnp.dot(
        msa_normed, averaged_lhs_weights, preferred_element_type=jnp.float32
    ).astype(jnp.bfloat16)
    right_msa = jnp.dot(
        msa_normed, averaged_rhs_weights, preferred_element_type=jnp.float32
    ).astype(jnp.bfloat16)
    right_send = right_msa.transpose(1, 2, 0).reshape(cols, hidden * seqs)
    left_send = left_msa.transpose(1, 0, 2).reshape(chips, cores * rows, seqs * hidden)
    payload = jnp.concatenate(
        [
            jnp.broadcast_to(right_send, (groups, chips) + right_send.shape),
            jnp.broadcast_to(left_send, (groups,) + left_send.shape),
        ],
        axis=2,
    ).reshape(groups * chips, cols + cores * rows, hidden * seqs)
    gathered = lax.all_to_all(payload, ("dap", "chip"), split_axis=0, concat_axis=0, tiled=True)
    gathered = gathered.reshape(groups, chips, cols + cores * rows, hidden * seqs)
    left_rows = lax.dynamic_index_in_dim(
        gathered[:, :, cols:], lax.axis_index("dap"), 0, keepdims=False
    )
    left_rows = (
        left_rows.reshape(chips, cores, rows, seqs, hidden)
        .transpose(1, 2, 0, 3, 4)
    )
    weight = mean_final_linear.reshape(hidden, hidden * pair_width)
    other_left = lax.dynamic_index_in_dim(left_rows, 1 - core, 0, keepdims=False)
    own_left = lax.dynamic_index_in_dim(left_rows, core, 0, keepdims=False)
    other_part = opm_rows(gathered, other_left, weight, depth, cols, jnp.bfloat16)
    arrived = lax.ppermute(other_part, "core", [(0, 1), (1, 0)])
    own_part = opm_rows(gathered, own_left, weight, depth, cols, jnp.float32)

    updated = (
        couple_embedding.astype(jnp.float32) + (own_part + arrived.astype(jnp.float32))
    ).astype(jnp.bfloat16)
    pair_normed = standardize_features(updated.astype(jnp.float32), couple_scale_vector).astype(
        jnp.bfloat16
    )
    left_tri = gated_operand(pair_normed, first_linear_map, first_sigmoid_factor)
    right_tri = gated_operand(pair_normed, second_linear_map, second_sigmoid_factor)
    gate = jax.nn.sigmoid(
        jnp.dot(pair_normed, final_sigmoid_factor, preferred_element_type=jnp.float32)
    )
    operands = jnp.concatenate(
        [left_tri.transpose(2, 0, 1), right_tri.transpose(2, 0, 1)], axis=1
    )
    operands = lax.all_to_all(operands, ALL, split_axis=0, concat_axis=0, tiled=True)
    left_full = operands[:, :rows].reshape(devices * rows, length)
    right_full = operands[:, rows:].reshape(devices * rows, length)
    mixed = lax.dot_general(
        left_full, right_full, (((1,), (1,)), ((), ())), preferred_element_type=jnp.float32
    ).astype(jnp.bfloat16)
    mixed_back = lax.all_to_all(
        mixed.reshape(devices, rows, length), ALL, split_axis=0, concat_axis=0, tiled=True
    )
    mixed_normed = standardize_features(
        mixed_back.astype(jnp.float32), trio_scale_vector[:, None, None], axis=0
    ).astype(jnp.bfloat16)
    output_term = lax.dot_general(
        mixed_normed, trio_final_linear, (((0,), (0,)), ((), ())), preferred_element_type=jnp.float32
    )
    return (updated.astype(jnp.float32) + gate * output_term).astype(jnp.bfloat16)


def solution(mesh):
    groups, lanes = mesh.shape["dap"], mesh.shape["bulk"]
    fine = Mesh(mesh.devices.reshape(groups, lanes // 2, 2), ALL)
    return jax.shard_map(
        body,
        mesh=fine,
        in_specs=(P(("chip", "core"), "dap", None), P(ALL, None, None)) + (P(),) * 12,
        out_specs=P(ALL, None, None),
        check_vma=False,
    )
```

```python
import functools

import jax
import jax.numpy as jnp
from jax import lax
from jax.experimental import pallas as pl
from jax.experimental.pallas import tpu as pltpu
from jax.sharding import Mesh, PartitionSpec as P

ALL = ("dap", "chip", "core")


def standardize_features(values, gain, axis=-1):
    center = values - jnp.mean(values, axis=axis, keepdims=True)
    spread = jnp.mean(center * center, axis=axis, keepdims=True)
    return center / jnp.sqrt(spread + 1e-05) * gain


MIB = 1024 * 1024


def ones_where(condition):
    return condition.astype(jnp.float32).astype(jnp.bfloat16)


def iota(shape, axis):
    return lax.broadcasted_iota(jnp.int32, shape, axis)


def msa_kernel(msa_ref, gain_ref, left_ref, right_ref, send_ref, block, sems):
    seqs, cols, features = msa_ref.shape
    hidden = left_ref.shape[0]
    width = hidden * seqs
    chips, rows_sent, _ = block.shape
    left_rows = rows_sent - cols
    pairs = width // hidden
    spread = ones_where(iota((hidden, width), 1) // seqs == iota((hidden, width), 0))
    right_copies = lax.dot_general(
        right_ref[...], spread, (((0,), (0,)), ((), ())), preferred_element_type=jnp.float32
    )
    right_lane = iota(right_copies.shape, 1) % seqs
    tiled = ones_where(iota((hidden, width), 1) % hidden == iota((hidden, width), 0))
    left_copies = lax.dot_general(
        left_ref[...], tiled, (((0,), (0,)), ((), ())), preferred_element_type=jnp.float32
    ).astype(jnp.bfloat16)
    own_lane = iota((cols, width), 1) // hidden == iota((cols, width), 0) // 2 % pairs
    place = (chips * left_rows, cols)
    target, source = iota(place, 0), iota(place, 1)
    same_pair = (target // left_rows == source // left_rows) & (
        target // seqs % 2 == source % 2
    )
    right = jnp.zeros((cols, width), jnp.float32)
    left = jnp.zeros((chips * left_rows, width), jnp.float32)
    for s in range(seqs):
        normed = standardize_features(msa_ref[s].astype(jnp.float32), gain_ref[...]).astype(
            jnp.bfloat16
        )
        right = right + jnp.dot(
            normed,
            jnp.where(right_lane == s, right_copies, 0.0).astype(jnp.bfloat16),
            preferred_element_type=jnp.float32,
        )
        products = jnp.dot(normed, left_copies, preferred_element_type=jnp.float32)
        left = left + jnp.dot(
            ones_where(same_pair & (target % seqs == s)),
            jnp.where(own_lane, products, 0.0).astype(jnp.bfloat16),
            preferred_element_type=jnp.float32,
        )
    right = right.astype(jnp.bfloat16)
    left = left.astype(jnp.bfloat16)
    for chip in range(chips):
        block[chip, :cols, :] = right
        block[chip, cols:, :] = left[chip * left_rows : (chip + 1) * left_rows]
    copies = [
        pltpu.make_async_copy(block, send_ref.at[pl.ds(group * chips, chips)], sems.at[group])
        for group in range(send_ref.shape[0] // chips)
    ]
    for copy in copies:
        copy.start()
    for copy in copies:
        copy.wait()


def whole(shape):
    return pl.BlockSpec(shape, lambda *_: (0,) * len(shape))


def msa_payload(msa, gain, left, right, groups, chips, left_rows):
    seqs, cols, features = msa.shape
    width = seqs * left.shape[1]
    operands = (msa, gain.reshape(1, features), left.T, right.T)
    return pl.pallas_call(
        msa_kernel,
        grid=(1,),
        in_specs=[whole(operand.shape) for operand in operands],
        out_specs=pl.BlockSpec(memory_space=pl.ANY),
        out_shape=jax.ShapeDtypeStruct((groups * chips, cols + left_rows, width), jnp.bfloat16),
        scratch_shapes=[
            pltpu.VMEM((chips, cols + left_rows, width), jnp.bfloat16),
            pltpu.SemaphoreType.DMA((groups,)),
        ],
        compiler_params=pltpu.CompilerParams(vmem_limit_bytes=58 * MIB),
    )(*operands)


def opm_kernel(
    own, place_ref, gathered_ref, weight_ref, out_ref, right_rows, left_block, left_rows, mixer, sems
):
    groups, cols, _ = right_rows.shape
    _, chips, _, width = gathered_ref.shape
    pairs, stacked, hidden = left_rows.shape
    seqs = width // hidden
    channels = weight_ref.shape[1] // hidden
    here = out_ref.shape[0] // 2
    copies = [
        pltpu.make_async_copy(
            gathered_ref.at[:, chip, pl.ds(0, cols), :],
            right_rows.at[:, :, pl.ds(chip * width, width)],
            sems.at[chip],
        )
        for chip in range(chips)
    ]
    left_copy = pltpu.make_async_copy(
        gathered_ref.at[place_ref[0], :, pl.ds(cols, 2 * seqs), :], left_block, sems.at[chips]
    )

    @pl.when(pl.program_id(0) == 0)
    def _():
        left_copy.start()
        for copy in copies:
            copy.start()
        left_copy.wait()
        half = place_ref[1] if own else 1 - place_ref[1]
        half = pl.multiple_of(half * (pairs * hidden), pairs * hidden)
        left = left_block[:, :, pl.ds(half, pairs * hidden)].reshape(stacked, pairs * hidden)
        for pair in range(pairs):
            left_rows[pair] = left[:, pair * hidden : (pair + 1) * hidden]

    step = 16 // seqs
    for pair in range(here):
        expanded = jnp.dot(
            left_rows[pl.program_id(0) * here + pair],
            weight_ref[...],
            preferred_element_type=jnp.float32,
        )
        for chip in range(chips):
            for row in range(2):
                start = (chip * 2 + row) * seqs
                column = (pair * 2 + row) * channels
                for d in range(0, hidden, step):
                    tile = jnp.concatenate(
                        [
                            expanded[start : start + seqs, k * channels : (k + 1) * channels]
                            for k in range(d, d + step)
                        ],
                        axis=0,
                    )
                    mixer[
                        chip * width + d * seqs : chip * width + (d + step) * seqs,
                        column : column + channels,
                    ] = tile.astype(jnp.bfloat16)

    @pl.when(pl.program_id(0) == 0)
    def _():
        for copy in copies:
            copy.wait()

    out = jnp.dot(
        right_rows[...].reshape(groups * cols, chips * width),
        mixer[...],
        preferred_element_type=jnp.float32,
    )
    for row in range(out_ref.shape[0]):
        out_ref[row] = out[:, row * channels : (row + 1) * channels].astype(out_ref.dtype)


def opm_rows(own, place, gathered, weight, cols, rows, step_rows=4):
    groups, chips, rows_sent, width = gathered.shape
    hidden = weight.shape[0]
    channels = weight.shape[1] // hidden
    seqs = width // hidden
    return pl.pallas_call(
        functools.partial(opm_kernel, own),
        grid=(rows // step_rows,),
        in_specs=[
            pl.BlockSpec(memory_space=pltpu.SMEM),
            pl.BlockSpec(memory_space=pl.ANY),
            whole(weight.shape),
        ],
        out_specs=pl.BlockSpec((step_rows, groups * cols, channels), lambda i: (i, 0, 0)),
        out_shape=jax.ShapeDtypeStruct((rows, groups * cols, channels), jnp.bfloat16),
        scratch_shapes=[
            pltpu.VMEM((groups, cols, chips * width), jnp.bfloat16),
            pltpu.VMEM((chips, 2 * seqs, width), jnp.bfloat16),
            pltpu.VMEM((rows // 2, chips * 2 * seqs, hidden), jnp.bfloat16),
            pltpu.VMEM((chips * width, step_rows * channels), jnp.bfloat16),
            pltpu.SemaphoreType.DMA((chips + 1,)),
        ],
        compiler_params=pltpu.CompilerParams(vmem_limit_bytes=24 * MIB),
        cost_estimate=pl.CostEstimate(
            flops=2 * rows * groups * cols * chips * width * channels,
            bytes_accessed=gathered.size * 2 + rows * groups * cols * channels * 2,
            transcendentals=0,
        ),
    )(place, gathered, weight)


def half_sigmoid(values):
    return 0.5 * jnp.tanh(0.5 * values) + 0.5


def pair_kernel(
    scale, pair_ref, own_ref, arrived_ref, gain_ref, *rest
):
    *weight_refs, updated_ref, normed_ref, send_ref, rows_buf, weight_buf = rest
    rows, cols, width = pair_ref.shape
    channels = weight_refs[0].shape[1]

    @pl.when(pl.program_id(0) == 0)
    def _():
        for k, weight_ref in enumerate(weight_refs):
            weight_buf[k * channels : (k + 1) * channels, :] = weight_ref[...].T

    for row in range(rows):
        updated = (
            pair_ref[row].astype(jnp.float32)
            + (own_ref[row].astype(jnp.float32) + arrived_ref[row].astype(jnp.float32)) * scale
        ).astype(jnp.bfloat16)
        updated_ref[row] = updated
        normed = standardize_features(updated.astype(jnp.float32), gain_ref[...]).astype(
            jnp.bfloat16
        )
        normed_ref[row] = normed
        products = lax.dot_general(
            weight_buf[...], normed, (((1,), (1,)), ((), ())), preferred_element_type=jnp.float32
        )
        for side in range(2):
            start = 2 * side * channels
            gated = products[start : start + channels] * half_sigmoid(
                products[start + channels : start + 2 * channels]
            )
            for lane in range(0, cols, 128):
                rows_buf[lane // 128, pl.ds(side * rows + row, channels, stride=2 * rows), :] = (
                    gated[:, lane : lane + 128]
                )
    for lane in range(0, cols, 128):
        send_ref[:, :, lane : lane + 128] = (
            rows_buf[lane // 128].reshape(channels, 2 * rows, 128).astype(jnp.bfloat16)
        )


def pair_operands(pair, own, arrived, gain, weights, scale):
    rows, length, width = pair.shape
    channels = weights[0].shape[1]
    cols = 256
    block = pl.BlockSpec((rows, cols, width), lambda i: (0, i, 0))
    return pl.pallas_call(
        functools.partial(pair_kernel, scale),
        grid=(length // cols,),
        in_specs=[
            block,
            block,
            block,
            pl.BlockSpec((1, width), lambda i: (0, 0)),
        ]
        + [whole(weight.shape) for weight in weights],
        out_specs=[
            block,
            block,
            pl.BlockSpec((channels, 2 * rows, cols), lambda i: (0, 0, i)),
        ],
        out_shape=[
            jax.ShapeDtypeStruct(pair.shape, jnp.bfloat16),
            jax.ShapeDtypeStruct(pair.shape, jnp.bfloat16),
            jax.ShapeDtypeStruct((channels, 2 * rows, length), jnp.bfloat16),
        ],
        scratch_shapes=[
            pltpu.VMEM((cols // 128, channels * 2 * rows, 128), jnp.float32),
            pltpu.VMEM((len(weights) * channels, width), jnp.bfloat16),
        ],
        compiler_params=pltpu.CompilerParams(vmem_limit_bytes=18 * MIB),
        cost_estimate=pl.CostEstimate(
            flops=8 * rows * length * width * channels,
            bytes_accessed=rows * length * width * 18,
            transcendentals=2 * rows * length * channels,
        ),
    )(pair, own, arrived, gain.reshape(1, width), *weights)


def result_kernel(mixed_ref, updated_ref, gate_ref, gain_ref, weight_ref, out_ref, rows_buf):
    channels, rows, cols = mixed_ref.shape
    for lane in range(0, cols, 128):
        values = mixed_ref[:, :, lane : lane + 128].astype(jnp.float32)
        center = values - jnp.mean(values, axis=0, keepdims=True)
        spread = jnp.mean(center * center, axis=0, keepdims=True)
        scaled = center * (1.0 / jnp.sqrt(spread + 1e-05))
        rows_buf[...] = scaled.reshape(channels * rows, 128)
        for row in range(rows):
            normed = (rows_buf[pl.ds(row, channels, stride=rows), :] * gain_ref[...]).astype(
                jnp.bfloat16
            )
            term = lax.dot_general(
                normed, weight_ref[...], (((0,), (0,)), ((), ())), preferred_element_type=jnp.float32
            )
            out_ref[row, lane : lane + 128, :] = (
                updated_ref[row, lane : lane + 128, :].astype(jnp.float32)
                + gate_ref[row, lane : lane + 128, :].astype(jnp.float32) * term
            ).astype(jnp.bfloat16)


def result_rows(mixed, updated, gate, gain, weight):
    channels, rows, length = mixed.shape
    width = weight.shape[1]
    cols = 256
    block = pl.BlockSpec((rows, cols, width), lambda i: (0, i, 0))
    return pl.pallas_call(
        result_kernel,
        grid=(length // cols,),
        in_specs=[
            pl.BlockSpec((channels, rows, cols), lambda i: (0, 0, i)),
            block,
            block,
            pl.BlockSpec((channels, 1), lambda i: (0, 0)),
            pl.BlockSpec(weight.shape, lambda i: (0, 0)),
        ],
        out_specs=block,
        out_shape=jax.ShapeDtypeStruct((rows, length, width), jnp.bfloat16),
        scratch_shapes=[pltpu.VMEM((channels * rows, 128), jnp.float32)],
        compiler_params=pltpu.CompilerParams(vmem_limit_bytes=14 * MIB),
        cost_estimate=pl.CostEstimate(
            flops=2 * rows * length * width * channels,
            bytes_accessed=rows * length * width * 10,
            transcendentals=0,
        ),
    )(mixed, updated, gate, gain.reshape(channels, 1), weight)


def body(
    stacked_relatives_tensor,
    couple_embedding,
    relatives_rescaler,
    averaged_lhs_weights,
    averaged_rhs_weights,
    mean_final_linear,
    couple_scale_vector,
    first_linear_map,
    first_sigmoid_factor,
    second_linear_map,
    second_sigmoid_factor,
    final_sigmoid_factor,
    trio_scale_vector,
    trio_final_linear,
):
    groups, chips, cores = (lax.axis_size(name) for name in ALL)
    devices = groups * chips * cores
    seqs, cols, features = stacked_relatives_tensor.shape
    hidden = averaged_lhs_weights.shape[1]
    depth = seqs * chips * cores
    rows, length, pair_width = couple_embedding.shape

    payload = msa_payload(
        stacked_relatives_tensor,
        relatives_rescaler,
        averaged_lhs_weights,
        averaged_rhs_weights,
        groups,
        chips,
        cores * rows,
    )
    gathered = lax.all_to_all(payload, ("dap", "chip"), split_axis=0, concat_axis=0, tiled=True)
    gathered = gathered.reshape(groups, chips, cols + cores * rows, hidden * seqs)
    weight = mean_final_linear.reshape(hidden, hidden * pair_width)
    place = jnp.stack([lax.axis_index("dap"), lax.axis_index("core")])
    other_part = opm_rows(False, place, gathered, weight, cols, rows)
    arrived = lax.ppermute(other_part, "core", [(0, 1), (1, 0)])
    own_part = opm_rows(True, place, gathered, weight, cols, rows)
    tri_weights = (
        first_linear_map, first_sigmoid_factor, second_linear_map, second_sigmoid_factor
    )
    updated, pair_normed, operands = pair_operands(
        couple_embedding, own_part, arrived, couple_scale_vector, tri_weights, 1.0 / depth
    )
    gate = jax.nn.sigmoid(
        jnp.dot(pair_normed, final_sigmoid_factor, preferred_element_type=jnp.float32)
    ).astype(jnp.bfloat16)
    operands = lax.all_to_all(operands, ALL, split_axis=0, concat_axis=0, tiled=True)
    left_full = operands[:, :rows].reshape(devices * rows, length)
    right_full = operands[:, rows:].reshape(devices * rows, length)
    mixed = lax.dot_general(
        left_full, right_full, (((1,), (1,)), ((), ())), preferred_element_type=jnp.float32
    ).astype(jnp.bfloat16)
    mixed_back = lax.all_to_all(
        mixed.reshape(devices, rows, length), ALL, split_axis=0, concat_axis=0, tiled=True
    )
    return result_rows(mixed_back, updated, gate, trio_scale_vector, trio_final_linear)


def solution(mesh):
    groups, lanes = mesh.shape["dap"], mesh.shape["bulk"]
    fine = Mesh(mesh.devices.reshape(groups, lanes // 2, 2), ALL)
    return jax.shard_map(
        body,
        mesh=fine,
        in_specs=(P(("chip", "core"), "dap", None), P(ALL, None, None)) + (P(),) * 12,
        out_specs=P(ALL, None, None),
        check_vma=False,
    )
```

```python
import functools

import jax
import jax.numpy as jnp
from jax import lax
from jax.experimental import pallas as pl
from jax.experimental.pallas import tpu as pltpu
from jax.sharding import Mesh, PartitionSpec as P

ALL = ("dap", "chip", "core")


def standardize_features(values, gain, axis=-1):
    center = values - jnp.mean(values, axis=axis, keepdims=True)
    spread = jnp.mean(center * center, axis=axis, keepdims=True)
    return center / jnp.sqrt(spread + 1e-05) * gain


MIB = 1024 * 1024


def ones_where(condition):
    return condition.astype(jnp.float32).astype(jnp.bfloat16)


def iota(shape, axis):
    return lax.broadcasted_iota(jnp.int32, shape, axis)


def msa_kernel(msa_ref, gain_ref, left_ref, right_ref, first_ref, second_ref, first, second, sems):
    seqs, cols, features = msa_ref.shape
    hidden = left_ref.shape[0]
    width = hidden * seqs
    chips, part, _ = second.shape
    left_rows = first.shape[1] - part
    pairs = width // hidden
    spread = ones_where(iota((hidden, width), 1) // seqs == iota((hidden, width), 0))
    right_copies = lax.dot_general(
        right_ref[...], spread, (((0,), (0,)), ((), ())), preferred_element_type=jnp.float32
    )
    right_lane = iota(right_copies.shape, 1) % seqs
    tiled = ones_where(iota((hidden, width), 1) % hidden == iota((hidden, width), 0))
    left_copies = lax.dot_general(
        left_ref[...], tiled, (((0,), (0,)), ((), ())), preferred_element_type=jnp.float32
    ).astype(jnp.bfloat16)
    own_lane = iota((cols, width), 1) // hidden == iota((cols, width), 0) // 2 % pairs
    place = (chips * left_rows, cols)
    target, source = iota(place, 0), iota(place, 1)
    same_pair = (target // left_rows == source // left_rows) & (
        target // seqs % 2 == source % 2
    )
    right = jnp.zeros((cols, width), jnp.float32)
    left = jnp.zeros((chips * left_rows, width), jnp.float32)
    for s in range(seqs):
        normed = standardize_features(msa_ref[s].astype(jnp.float32), gain_ref[...]).astype(
            jnp.bfloat16
        )
        right = right + jnp.dot(
            normed,
            jnp.where(right_lane == s, right_copies, 0.0).astype(jnp.bfloat16),
            preferred_element_type=jnp.float32,
        )
        products = jnp.dot(normed, left_copies, preferred_element_type=jnp.float32)
        left = left + jnp.dot(
            ones_where(same_pair & (target % seqs == s)),
            jnp.where(own_lane, products, 0.0).astype(jnp.bfloat16),
            preferred_element_type=jnp.float32,
        )
    right = right.astype(jnp.bfloat16)
    left = left.astype(jnp.bfloat16)
    for chip in range(chips):
        first[chip, :part, :] = right[:part]
        first[chip, part:, :] = left[chip * left_rows : (chip + 1) * left_rows]
        second[chip] = right[part:]
    copies = [
        pltpu.make_async_copy(
            block, send_ref.at[pl.ds(group * chips, chips)], sems.at[k, group]
        )
        for k, (block, send_ref) in enumerate(((first, first_ref), (second, second_ref)))
        for group in range(first_ref.shape[0] // chips)
    ]
    for copy in copies:
        copy.start()
    for copy in copies:
        copy.wait()


def whole(shape):
    return pl.BlockSpec(shape, lambda *_: (0,) * len(shape))


def msa_payload(msa, gain, left, right, groups, chips, left_rows):
    seqs, cols, features = msa.shape
    width = seqs * left.shape[1]
    operands = (msa, gain.reshape(1, features), left.T, right.T)
    return pl.pallas_call(
        msa_kernel,
        grid=(1,),
        in_specs=[whole(operand.shape) for operand in operands],
        out_specs=[pl.BlockSpec(memory_space=pl.ANY)] * 2,
        out_shape=[
            jax.ShapeDtypeStruct((groups * chips, count, width), jnp.bfloat16)
            for count in (cols // 2 + left_rows, cols // 2)
        ],
        scratch_shapes=[
            pltpu.VMEM((chips, cols // 2 + left_rows, width), jnp.bfloat16),
            pltpu.VMEM((chips, cols // 2, width), jnp.bfloat16),
            pltpu.SemaphoreType.DMA((2, groups)),
        ],
        compiler_params=pltpu.CompilerParams(vmem_limit_bytes=58 * MIB),
    )(*operands)


def opm_kernel(
    own, place_ref, gathered_ref, left_ref, weight_ref, out_ref, right_rows, left_block, left_rows, mixer, sems
):
    groups, cols, _ = right_rows.shape
    _, chips, _, width = gathered_ref.shape
    pairs, stacked, hidden = left_rows.shape
    seqs = width // hidden
    channels = weight_ref.shape[1] // hidden
    here = out_ref.shape[0] // 2
    copies = [
        pltpu.make_async_copy(
            gathered_ref.at[:, chip, pl.ds(0, cols), :],
            right_rows.at[:, :, pl.ds(chip * width, width)],
            sems.at[chip],
        )
        for chip in range(chips)
    ]
    left_copy = pltpu.make_async_copy(
        left_ref.at[place_ref[0], :, pl.ds(left_ref.shape[2] - 2 * seqs, 2 * seqs), :],
        left_block,
        sems.at[chips],
    )

    @pl.when(pl.program_id(0) == 0)
    def _():
        left_copy.start()
        for copy in copies:
            copy.start()
        left_copy.wait()
        half = place_ref[1] if own else 1 - place_ref[1]
        half = pl.multiple_of(half * (pairs * hidden), pairs * hidden)
        left = left_block[:, :, pl.ds(half, pairs * hidden)].reshape(stacked, pairs * hidden)
        for pair in range(pairs):
            left_rows[pair] = left[:, pair * hidden : (pair + 1) * hidden]

    step = 16 // seqs
    for pair in range(here):
        expanded = jnp.dot(
            left_rows[pl.program_id(0) * here + pair],
            weight_ref[...],
            preferred_element_type=jnp.float32,
        )
        for chip in range(chips):
            for row in range(2):
                start = (chip * 2 + row) * seqs
                column = (pair * 2 + row) * channels
                for d in range(0, hidden, step):
                    tile = jnp.concatenate(
                        [
                            expanded[start : start + seqs, k * channels : (k + 1) * channels]
                            for k in range(d, d + step)
                        ],
                        axis=0,
                    )
                    mixer[
                        chip * width + d * seqs : chip * width + (d + step) * seqs,
                        column : column + channels,
                    ] = tile.astype(jnp.bfloat16)

    @pl.when(pl.program_id(0) == 0)
    def _():
        for copy in copies:
            copy.wait()

    out = jnp.dot(
        right_rows[...].reshape(groups * cols, chips * width),
        mixer[...],
        preferred_element_type=jnp.float32,
    )
    for row in range(out_ref.shape[0]):
        out_ref[row] = out[:, row * channels : (row + 1) * channels].astype(out_ref.dtype)


def opm_rows(own, place, gathered, left, weight, cols, rows, step_rows=4):
    groups, chips, rows_sent, width = gathered.shape
    hidden = weight.shape[0]
    channels = weight.shape[1] // hidden
    seqs = width // hidden
    return pl.pallas_call(
        functools.partial(opm_kernel, own),
        grid=(rows // step_rows,),
        in_specs=[
            pl.BlockSpec(memory_space=pltpu.SMEM),
            pl.BlockSpec(memory_space=pl.ANY),
            pl.BlockSpec(memory_space=pl.ANY),
            whole(weight.shape),
        ],
        out_specs=pl.BlockSpec((step_rows, groups * cols, channels), lambda i: (i, 0, 0)),
        out_shape=jax.ShapeDtypeStruct((rows, groups * cols, channels), jnp.bfloat16),
        scratch_shapes=[
            pltpu.VMEM((groups, cols, chips * width), jnp.bfloat16),
            pltpu.VMEM((chips, 2 * seqs, width), jnp.bfloat16),
            pltpu.VMEM((rows // 2, chips * 2 * seqs, hidden), jnp.bfloat16),
            pltpu.VMEM((chips * width, step_rows * channels), jnp.bfloat16),
            pltpu.SemaphoreType.DMA((chips + 1,)),
        ],
        compiler_params=pltpu.CompilerParams(vmem_limit_bytes=24 * MIB),
        cost_estimate=pl.CostEstimate(
            flops=2 * rows * groups * cols * chips * width * channels,
            bytes_accessed=gathered.size * 2 + rows * groups * cols * channels * 2,
            transcendentals=0,
        ),
    )(place, gathered, left, weight)


def half_sigmoid(values):
    return 0.5 * jnp.tanh(0.5 * values) + 0.5


def pair_kernel(
    scale, pair_ref, own_ref, arrived_ref, gain_ref, *rest
):
    *weight_refs, updated_ref, normed_ref, send_ref, rows_buf, weight_buf = rest
    rows, cols, width = own_ref.shape
    channels = weight_refs[0].shape[1]

    @pl.when(pl.program_id(0) == 0)
    def _():
        for k, weight_ref in enumerate(weight_refs):
            weight_buf[k * channels : (k + 1) * channels, :] = weight_ref[...].T

    for row in range(rows):
        updated = (
            pair_ref[row].reshape(cols, width).astype(jnp.float32)
            + (own_ref[row].astype(jnp.float32) + arrived_ref[row].astype(jnp.float32)) * scale
        ).astype(jnp.bfloat16)
        updated_ref[row] = updated
        normed = standardize_features(updated.astype(jnp.float32), gain_ref[...]).astype(
            jnp.bfloat16
        )
        normed_ref[row] = normed
        products = lax.dot_general(
            weight_buf[...], normed, (((1,), (1,)), ((), ())), preferred_element_type=jnp.float32
        )
        for side in range(2):
            start = 2 * side * channels
            gated = products[start : start + channels] * half_sigmoid(
                products[start + channels : start + 2 * channels]
            )
            for lane in range(0, cols, 128):
                rows_buf[lane // 128, pl.ds(side * rows + row, channels, stride=2 * rows), :] = (
                    gated[:, lane : lane + 128]
                )
    for lane in range(0, cols, 128):
        send_ref[:, :, lane : lane + 128] = (
            rows_buf[lane // 128].reshape(channels, 2 * rows, 128).astype(jnp.bfloat16)
        )


def pair_operands(half, pair, own, arrived, gain, weights, scale):
    rows, length, width = own.shape
    groups = pair.shape[1]
    part = length // groups
    channels = weights[0].shape[1]
    cols = 256
    block = pl.BlockSpec((rows, cols, width), lambda i: (0, i, 0))
    return pl.pallas_call(
        functools.partial(pair_kernel, scale),
        grid=(length // cols,),
        in_specs=[
            pl.BlockSpec((rows, cols // part, part, width), lambda i: (0, i, half, 0)),
            block,
            block,
            pl.BlockSpec((1, width), lambda i: (0, 0)),
        ]
        + [whole(weight.shape) for weight in weights],
        out_specs=[
            block,
            block,
            pl.BlockSpec((channels, 2 * rows, cols), lambda i: (0, 0, i)),
        ],
        out_shape=[
            jax.ShapeDtypeStruct(own.shape, jnp.bfloat16),
            jax.ShapeDtypeStruct(own.shape, jnp.bfloat16),
            jax.ShapeDtypeStruct((channels, 2 * rows, length), jnp.bfloat16),
        ],
        scratch_shapes=[
            pltpu.VMEM((cols // 128, channels * 2 * rows, 128), jnp.float32),
            pltpu.VMEM((len(weights) * channels, width), jnp.bfloat16),
        ],
        compiler_params=pltpu.CompilerParams(vmem_limit_bytes=18 * MIB),
        cost_estimate=pl.CostEstimate(
            flops=8 * rows * length * width * channels,
            bytes_accessed=rows * length * width * 18,
            transcendentals=2 * rows * length * channels,
        ),
    )(pair, own, arrived, gain.reshape(1, width), *weights)


def result_kernel(mixed_ref, *refs):
    *halves, gain_ref, weight_ref, out_ref, rows_buf = refs
    channels, rows, cols = mixed_ref.shape
    for lane in range(0, cols, 128):
        values = mixed_ref[:, :, lane : lane + 128].astype(jnp.float32)
        center = values - jnp.mean(values, axis=0, keepdims=True)
        spread = jnp.mean(center * center, axis=0, keepdims=True)
        scaled = center * (1.0 / jnp.sqrt(spread + 1e-05))
        rows_buf[...] = scaled.reshape(channels * rows, 128)
        for row in range(rows):
            normed = (rows_buf[pl.ds(row, channels, stride=rows), :] * gain_ref[...]).astype(
                jnp.bfloat16
            )
            term = lax.dot_general(
                normed, weight_ref[...], (((0,), (0,)), ((), ())), preferred_element_type=jnp.float32
            )
            for half in range(2):
                updated_ref, gate_ref = halves[2 * half : 2 * half + 2]
                place = pl.ds(lane // 2, 64)
                out_ref[row, lane + 64 * half : lane + 64 * half + 64, :] = (
                    updated_ref[row, place, :].astype(jnp.float32)
                    + gate_ref[row, place, :].astype(jnp.float32)
                    * term[64 * half : 64 * half + 64]
                ).astype(jnp.bfloat16)


def result_rows(mixed, halves, gain, weight):
    channels, rows, length = mixed.shape
    width = weight.shape[1]
    cols = 256
    half_block = pl.BlockSpec((rows, cols // 2, width), lambda i: (0, i, 0))
    return pl.pallas_call(
        result_kernel,
        grid=(length // cols,),
        in_specs=[pl.BlockSpec((channels, rows, cols), lambda i: (0, 0, i))]
        + [half_block] * len(halves)
        + [whole((channels, 1)), whole(weight.shape)],
        out_specs=pl.BlockSpec((rows, cols, width), lambda i: (0, i, 0)),
        out_shape=jax.ShapeDtypeStruct((rows, length, width), jnp.bfloat16),
        scratch_shapes=[pltpu.VMEM((channels * rows, 128), jnp.float32)],
        compiler_params=pltpu.CompilerParams(vmem_limit_bytes=14 * MIB),
        cost_estimate=pl.CostEstimate(
            flops=2 * rows * length * width * channels,
            bytes_accessed=rows * length * width * 8,
            transcendentals=0,
        ),
    )(mixed, *halves, gain.reshape(channels, 1), weight)


def body(
    stacked_relatives_tensor,
    couple_embedding,
    relatives_rescaler,
    averaged_lhs_weights,
    averaged_rhs_weights,
    mean_final_linear,
    couple_scale_vector,
    first_linear_map,
    first_sigmoid_factor,
    second_linear_map,
    second_sigmoid_factor,
    final_sigmoid_factor,
    trio_scale_vector,
    trio_final_linear,
):
    groups, chips, cores = (lax.axis_size(name) for name in ALL)
    devices = groups * chips * cores
    seqs, cols, features = stacked_relatives_tensor.shape
    hidden = averaged_lhs_weights.shape[1]
    depth = seqs * chips * cores
    rows, length, pair_width = couple_embedding.shape

    payloads = msa_payload(
        stacked_relatives_tensor,
        relatives_rescaler,
        averaged_lhs_weights,
        averaged_rhs_weights,
        groups,
        chips,
        cores * rows,
    )
    part = cols // 2
    gathered = [
        lax.all_to_all(
            payload, ("dap", "chip"), split_axis=0, concat_axis=0, tiled=True
        ).reshape(groups, chips, *payload.shape[1:])
        for payload in payloads
    ]
    weight = mean_final_linear.reshape(hidden, hidden * pair_width)
    place = jnp.stack([lax.axis_index("dap"), lax.axis_index("core")])
    pair = couple_embedding.reshape(rows, groups, cols, pair_width)
    tri_weights = (
        first_linear_map, first_sigmoid_factor, second_linear_map, second_sigmoid_factor
    )
    halves, operands = [], []
    for half in range(2):
        other_part = opm_rows(False, place, gathered[half], gathered[0], weight, part, rows)
        arrived = lax.ppermute(other_part, "core", [(0, 1), (1, 0)])
        own_part = opm_rows(True, place, gathered[half], gathered[0], weight, part, rows)
        updated, pair_normed, send = pair_operands(
            half, pair, own_part, arrived, couple_scale_vector, tri_weights, 1.0 / depth
        )
        gate = jax.nn.sigmoid(
            jnp.dot(pair_normed, final_sigmoid_factor, preferred_element_type=jnp.float32)
        ).astype(jnp.bfloat16)
        halves += [updated, gate]
        operands.append(lax.all_to_all(send, ALL, split_axis=0, concat_axis=0, tiled=True))
    mixed = sum(
        lax.dot_general(
            operand[:, :rows].reshape(devices * rows, length // 2),
            operand[:, rows:].reshape(devices * rows, length // 2),
            (((1,), (1,)), ((), ())),
            preferred_element_type=jnp.float32,
        )
        for operand in operands
    ).astype(jnp.bfloat16)
    mixed_back = lax.all_to_all(
        mixed.reshape(devices, rows, length), ALL, split_axis=0, concat_axis=0, tiled=True
    )
    return result_rows(mixed_back, halves, trio_scale_vector, trio_final_linear)


def solution(mesh):
    groups, lanes = mesh.shape["dap"], mesh.shape["bulk"]
    fine = Mesh(mesh.devices.reshape(groups, lanes // 2, 2), ALL)
    return jax.shard_map(
        body,
        mesh=fine,
        in_specs=(P(("chip", "core"), "dap", None), P(ALL, None, None)) + (P(),) * 12,
        out_specs=P(ALL, None, None),
        check_vma=False,
    )
```

```python
import functools

import jax
import jax.numpy as jnp
from jax import lax
from jax.experimental import pallas as pl
from jax.experimental.pallas import tpu as pltpu
from jax.sharding import Mesh, PartitionSpec as P

ALL = ("dap", "chip", "core")


def standardize_features(values, gain, axis=-1):
    center = values - jnp.mean(values, axis=axis, keepdims=True)
    spread = jnp.mean(center * center, axis=axis, keepdims=True)
    return center / jnp.sqrt(spread + 1e-05) * gain


MIB = 1024 * 1024


def ones_where(condition):
    return condition.astype(jnp.float32).astype(jnp.bfloat16)


def iota(shape, axis):
    return lax.broadcasted_iota(jnp.int32, shape, axis)


def msa_kernel(msa_ref, gain_ref, left_ref, right_ref, first_ref, second_ref, first, second, sems):
    seqs, cols, features = msa_ref.shape
    hidden = left_ref.shape[0]
    width = hidden * seqs
    chips, part, _ = second.shape
    left_rows = first.shape[1] - part
    pairs = width // hidden
    spread = ones_where(iota((hidden, width), 1) // seqs == iota((hidden, width), 0))
    right_copies = lax.dot_general(
        right_ref[...], spread, (((0,), (0,)), ((), ())), preferred_element_type=jnp.float32
    )
    right_lane = iota(right_copies.shape, 1) % seqs
    tiled = ones_where(iota((hidden, width), 1) % hidden == iota((hidden, width), 0))
    left_copies = lax.dot_general(
        left_ref[...], tiled, (((0,), (0,)), ((), ())), preferred_element_type=jnp.float32
    ).astype(jnp.bfloat16)
    own_lane = iota((cols, width), 1) // hidden == iota((cols, width), 0) // 2 % pairs
    place = (chips * left_rows, cols)
    target, source = iota(place, 0), iota(place, 1)
    same_pair = (target // left_rows == source // left_rows) & (
        target // seqs % 2 == source % 2
    )
    right = jnp.zeros((cols, width), jnp.float32)
    left = jnp.zeros((chips * left_rows, width), jnp.float32)
    for s in range(seqs):
        normed = standardize_features(msa_ref[s].astype(jnp.float32), gain_ref[...]).astype(
            jnp.bfloat16
        )
        right = right + jnp.dot(
            normed,
            jnp.where(right_lane == s, right_copies, 0.0).astype(jnp.bfloat16),
            preferred_element_type=jnp.float32,
        )
        products = jnp.dot(normed, left_copies, preferred_element_type=jnp.float32)
        left = left + jnp.dot(
            ones_where(same_pair & (target % seqs == s)),
            jnp.where(own_lane, products, 0.0).astype(jnp.bfloat16),
            preferred_element_type=jnp.float32,
        )
    right = right.astype(jnp.bfloat16)
    left = left.astype(jnp.bfloat16)
    for chip in range(chips):
        first[chip, :part, :] = right[:part]
        first[chip, part:, :] = left[chip * left_rows : (chip + 1) * left_rows]
        second[chip] = right[part:]
    copies = [
        pltpu.make_async_copy(
            block, send_ref.at[pl.ds(group * chips, chips)], sems.at[k, group]
        )
        for k, (block, send_ref) in enumerate(((first, first_ref), (second, second_ref)))
        for group in range(first_ref.shape[0] // chips)
    ]
    for copy in copies:
        copy.start()
    for copy in copies:
        copy.wait()


def whole(shape):
    return pl.BlockSpec(shape, lambda *_: (0,) * len(shape))


def msa_payload(msa, gain, left, right, groups, chips, left_rows):
    seqs, cols, features = msa.shape
    width = seqs * left.shape[1]
    operands = (msa, gain.reshape(1, features), left.T, right.T)
    return pl.pallas_call(
        msa_kernel,
        grid=(1,),
        in_specs=[whole(operand.shape) for operand in operands],
        out_specs=[pl.BlockSpec(memory_space=pl.ANY)] * 2,
        out_shape=[
            jax.ShapeDtypeStruct((groups * chips, count, width), jnp.bfloat16)
            for count in (cols // 2 + left_rows, cols // 2)
        ],
        scratch_shapes=[
            pltpu.VMEM((chips, cols // 2 + left_rows, width), jnp.bfloat16),
            pltpu.VMEM((chips, cols // 2, width), jnp.bfloat16),
            pltpu.SemaphoreType.DMA((2, groups)),
        ],
        compiler_params=pltpu.CompilerParams(vmem_limit_bytes=58 * MIB),
    )(*operands)


def opm_kernel(
    own, place_ref, gathered_ref, left_ref, weight_ref, out_ref, right_rows, left_block, left_rows, mixer, sems
):
    groups, cols, _ = right_rows.shape
    _, chips, _, width = gathered_ref.shape
    pairs, stacked, hidden = left_rows.shape
    seqs = width // hidden
    channels = weight_ref.shape[1] // hidden
    here = out_ref.shape[0] // 2
    copies = [
        pltpu.make_async_copy(
            gathered_ref.at[:, chip, pl.ds(0, cols), :],
            right_rows.at[:, :, pl.ds(chip * width, width)],
            sems.at[chip],
        )
        for chip in range(chips)
    ]
    left_copy = pltpu.make_async_copy(
        left_ref.at[place_ref[0], :, pl.ds(left_ref.shape[2] - 2 * seqs, 2 * seqs), :],
        left_block,
        sems.at[chips],
    )

    @pl.when(pl.program_id(0) == 0)
    def _():
        left_copy.start()
        for copy in copies:
            copy.start()
        left_copy.wait()
        half = place_ref[1] if own else 1 - place_ref[1]
        half = pl.multiple_of(half * (pairs * hidden), pairs * hidden)
        left = left_block[:, :, pl.ds(half, pairs * hidden)].reshape(stacked, pairs * hidden)
        for pair in range(pairs):
            left_rows[pair] = left[:, pair * hidden : (pair + 1) * hidden]

    step = 16 // seqs
    for pair in range(here):
        expanded = jnp.dot(
            left_rows[pl.program_id(0) * here + pair],
            weight_ref[...],
            preferred_element_type=jnp.float32,
        )
        for chip in range(chips):
            for row in range(2):
                start = (chip * 2 + row) * seqs
                column = (pair * 2 + row) * channels
                for d in range(0, hidden, step):
                    tile = jnp.concatenate(
                        [
                            expanded[start : start + seqs, k * channels : (k + 1) * channels]
                            for k in range(d, d + step)
                        ],
                        axis=0,
                    )
                    mixer[
                        chip * width + d * seqs : chip * width + (d + step) * seqs,
                        column : column + channels,
                    ] = tile.astype(jnp.bfloat16)

    @pl.when(pl.program_id(0) == 0)
    def _():
        for copy in copies:
            copy.wait()

    out = jnp.dot(
        right_rows[...].reshape(groups * cols, chips * width),
        mixer[...],
        preferred_element_type=jnp.float32,
    )
    for row in range(out_ref.shape[0]):
        out_ref[row] = out[:, row * channels : (row + 1) * channels].astype(out_ref.dtype)


def opm_rows(own, place, gathered, left, weight, cols, rows, step_rows=4):
    groups, chips, rows_sent, width = gathered.shape
    hidden = weight.shape[0]
    channels = weight.shape[1] // hidden
    seqs = width // hidden
    return pl.pallas_call(
        functools.partial(opm_kernel, own),
        grid=(rows // step_rows,),
        in_specs=[
            pl.BlockSpec(memory_space=pltpu.SMEM),
            pl.BlockSpec(memory_space=pl.ANY),
            pl.BlockSpec(memory_space=pl.ANY),
            whole(weight.shape),
        ],
        out_specs=pl.BlockSpec((step_rows, groups * cols, channels), lambda i: (i, 0, 0)),
        out_shape=jax.ShapeDtypeStruct((rows, groups * cols, channels), jnp.bfloat16),
        scratch_shapes=[
            pltpu.VMEM((groups, cols, chips * width), jnp.bfloat16),
            pltpu.VMEM((chips, 2 * seqs, width), jnp.bfloat16),
            pltpu.VMEM((rows // 2, chips * 2 * seqs, hidden), jnp.bfloat16),
            pltpu.VMEM((chips * width, step_rows * channels), jnp.bfloat16),
            pltpu.SemaphoreType.DMA((chips + 1,)),
        ],
        compiler_params=pltpu.CompilerParams(vmem_limit_bytes=24 * MIB),
        cost_estimate=pl.CostEstimate(
            flops=2 * rows * groups * cols * chips * width * channels,
            bytes_accessed=gathered.size * 2 + rows * groups * cols * channels * 2,
            transcendentals=0,
        ),
    )(place, gathered, left, weight)


def half_sigmoid(values):
    return 0.5 * jnp.tanh(0.5 * values) + 0.5


def pair_kernel(
    scale, pair_ref, own_ref, arrived_ref, gain_ref, *rest
):
    *weight_refs, updated_ref, normed_ref, send_ref, rows_buf, weight_buf = rest
    rows, cols, width = own_ref.shape
    channels = weight_refs[0].shape[1]

    @pl.when(pl.program_id(0) == 0)
    def _():
        for k, weight_ref in enumerate(weight_refs):
            weight_buf[k * channels : (k + 1) * channels, :] = weight_ref[...].T

    for row in range(rows):
        updated = (
            pair_ref[row].reshape(cols, width).astype(jnp.float32)
            + (own_ref[row].astype(jnp.float32) + arrived_ref[row].astype(jnp.float32)) * scale
        ).astype(jnp.bfloat16)
        updated_ref[row] = updated
        normed = standardize_features(updated.astype(jnp.float32), gain_ref[...]).astype(
            jnp.bfloat16
        )
        normed_ref[row] = normed
        products = lax.dot_general(
            weight_buf[...], normed, (((1,), (1,)), ((), ())), preferred_element_type=jnp.float32
        )
        for side in range(2):
            start = 2 * side * channels
            gated = products[start : start + channels] * half_sigmoid(
                products[start + channels : start + 2 * channels]
            )
            for lane in range(0, cols, 128):
                rows_buf[lane // 128, pl.ds(side * rows + row, channels, stride=2 * rows), :] = (
                    gated[:, lane : lane + 128]
                )
    for lane in range(0, cols, 128):
        send_ref[:, :, lane : lane + 128] = (
            rows_buf[lane // 128].reshape(channels, 2 * rows, 128).astype(jnp.bfloat16)
        )


def pair_operands(half, pair, own, arrived, gain, weights, scale):
    rows, length, width = own.shape
    groups = pair.shape[1]
    part = length // groups
    channels = weights[0].shape[1]
    cols = 256
    block = pl.BlockSpec((rows, cols, width), lambda i: (0, i, 0))
    return pl.pallas_call(
        functools.partial(pair_kernel, scale),
        grid=(length // cols,),
        in_specs=[
            pl.BlockSpec((rows, cols // part, part, width), lambda i: (0, i, half, 0)),
            block,
            block,
            pl.BlockSpec((1, width), lambda i: (0, 0)),
        ]
        + [whole(weight.shape) for weight in weights],
        out_specs=[
            block,
            block,
            pl.BlockSpec((channels, 2 * rows, cols), lambda i: (0, 0, i)),
        ],
        out_shape=[
            jax.ShapeDtypeStruct(own.shape, jnp.bfloat16),
            jax.ShapeDtypeStruct(own.shape, jnp.bfloat16),
            jax.ShapeDtypeStruct((channels, 2 * rows, length), jnp.bfloat16),
        ],
        scratch_shapes=[
            pltpu.VMEM((cols // 128, channels * 2 * rows, 128), jnp.float32),
            pltpu.VMEM((len(weights) * channels, width), jnp.bfloat16),
        ],
        compiler_params=pltpu.CompilerParams(vmem_limit_bytes=18 * MIB),
        cost_estimate=pl.CostEstimate(
            flops=8 * rows * length * width * channels,
            bytes_accessed=rows * length * width * 18,
            transcendentals=2 * rows * length * channels,
        ),
    )(pair, own, arrived, gain.reshape(1, width), *weights)


def result_kernel(mixed_ref, *refs):
    *halves, gain_ref, weight_ref, out_ref, rows_buf = refs
    channels, rows, cols = mixed_ref.shape
    for lane in range(0, cols, 128):
        values = mixed_ref[:, :, lane : lane + 128].astype(jnp.float32)
        center = values - jnp.mean(values, axis=0, keepdims=True)
        spread = jnp.mean(center * center, axis=0, keepdims=True)
        scaled = center * (1.0 / jnp.sqrt(spread + 1e-05))
        rows_buf[...] = scaled.reshape(channels * rows, 128)
        normed = jnp.concatenate(
            [rows_buf[pl.ds(row, channels, stride=rows), :] * gain_ref[...] for row in range(rows)],
            axis=1,
        ).astype(jnp.bfloat16)
        term = lax.dot_general(
            normed, weight_ref[...], (((0,), (0,)), ((), ())), preferred_element_type=jnp.float32
        ).reshape(rows, 128, -1)
        for half in range(2):
            updated_ref, gate_ref = halves[2 * half : 2 * half + 2]
            place = pl.ds(lane // 2, 64)
            out_ref[:, lane + 64 * half : lane + 64 * half + 64, :] = (
                updated_ref[:, place, :].astype(jnp.float32)
                + gate_ref[:, place, :].astype(jnp.float32)
                * term[:, 64 * half : 64 * half + 64]
            ).astype(jnp.bfloat16)


def result_rows(mixed, halves, gain, weight):
    channels, rows, length = mixed.shape
    width = weight.shape[1]
    cols = 256
    half_block = pl.BlockSpec((rows, cols // 2, width), lambda i: (0, i, 0))
    return pl.pallas_call(
        result_kernel,
        grid=(length // cols,),
        in_specs=[pl.BlockSpec((channels, rows, cols), lambda i: (0, 0, i))]
        + [half_block] * len(halves)
        + [whole((channels, 1)), whole(weight.shape)],
        out_specs=pl.BlockSpec((rows, cols, width), lambda i: (0, i, 0)),
        out_shape=jax.ShapeDtypeStruct((rows, length, width), jnp.bfloat16),
        scratch_shapes=[pltpu.VMEM((channels * rows, 128), jnp.float32)],
        compiler_params=pltpu.CompilerParams(vmem_limit_bytes=62 * MIB),
        cost_estimate=pl.CostEstimate(
            flops=2 * rows * length * width * channels,
            bytes_accessed=rows * length * width * 8,
            transcendentals=0,
        ),
    )(mixed, *halves, gain.reshape(channels, 1), weight)


def body(
    stacked_relatives_tensor,
    couple_embedding,
    relatives_rescaler,
    averaged_lhs_weights,
    averaged_rhs_weights,
    mean_final_linear,
    couple_scale_vector,
    first_linear_map,
    first_sigmoid_factor,
    second_linear_map,
    second_sigmoid_factor,
    final_sigmoid_factor,
    trio_scale_vector,
    trio_final_linear,
):
    groups, chips, cores = (lax.axis_size(name) for name in ALL)
    devices = groups * chips * cores
    seqs, cols, features = stacked_relatives_tensor.shape
    hidden = averaged_lhs_weights.shape[1]
    depth = seqs * chips * cores
    rows, length, pair_width = couple_embedding.shape

    payloads = msa_payload(
        stacked_relatives_tensor,
        relatives_rescaler,
        averaged_lhs_weights,
        averaged_rhs_weights,
        groups,
        chips,
        cores * rows,
    )
    part = cols // 2
    gathered = [
        lax.all_to_all(
            payload, ("dap", "chip"), split_axis=0, concat_axis=0, tiled=True
        ).reshape(groups, chips, *payload.shape[1:])
        for payload in payloads
    ]
    weight = mean_final_linear.reshape(hidden, hidden * pair_width)
    place = jnp.stack([lax.axis_index("dap"), lax.axis_index("core")])
    pair = couple_embedding.reshape(rows, groups, cols, pair_width)
    tri_weights = (
        first_linear_map, first_sigmoid_factor, second_linear_map, second_sigmoid_factor
    )
    halves, operands = [], []
    for half in range(2):
        other_part = opm_rows(False, place, gathered[half], gathered[0], weight, part, rows)
        arrived = lax.ppermute(other_part, "core", [(0, 1), (1, 0)])
        own_part = opm_rows(True, place, gathered[half], gathered[0], weight, part, rows)
        updated, pair_normed, send = pair_operands(
            half, pair, own_part, arrived, couple_scale_vector, tri_weights, 1.0 / depth
        )
        gate = jax.nn.sigmoid(
            jnp.dot(pair_normed, final_sigmoid_factor, preferred_element_type=jnp.float32)
        ).astype(jnp.bfloat16)
        halves += [updated, gate]
        operands.append(lax.all_to_all(send, ALL, split_axis=0, concat_axis=0, tiled=True))
    products = [
        functools.partial(
            lax.dot_general,
            operand[:, :rows].reshape(devices * rows, length // 2),
            operand[:, rows:].reshape(devices * rows, length // 2),
            (((1,), (1,)), ((), ())),
            preferred_element_type=jnp.float32,
        )
        for operand in operands
    ]
    first_half = lax.optimization_barrier(products[0]().astype(jnp.bfloat16))
    mixed = (first_half.astype(jnp.float32) + products[1]()).astype(jnp.bfloat16)
    mixed_back = lax.all_to_all(
        mixed.reshape(devices, rows, length), ALL, split_axis=0, concat_axis=0, tiled=True
    )
    return result_rows(mixed_back, halves, trio_scale_vector, trio_final_linear)


def solution(mesh):
    groups, lanes = mesh.shape["dap"], mesh.shape["bulk"]
    fine = Mesh(mesh.devices.reshape(groups, lanes // 2, 2), ALL)
    return jax.shard_map(
        body,
        mesh=fine,
        in_specs=(P(("chip", "core"), "dap", None), P(ALL, None, None)) + (P(),) * 12,
        out_specs=P(ALL, None, None),
        check_vma=False,
    )
```

```python
import functools

import jax
import jax.numpy as jnp
from jax import lax
from jax.experimental import pallas as pl
from jax.experimental.pallas import tpu as pltpu
from jax.sharding import Mesh, PartitionSpec as P

ALL = ("dap", "chip", "core")


def standardize_features(values, gain, axis=-1):
    center = values - jnp.mean(values, axis=axis, keepdims=True)
    spread = jnp.mean(center * center, axis=axis, keepdims=True)
    return center / jnp.sqrt(spread + 1e-05) * gain


MIB = 1024 * 1024


def ones_where(condition):
    return condition.astype(jnp.float32).astype(jnp.bfloat16)


def iota(shape, axis):
    return lax.broadcasted_iota(jnp.int32, shape, axis)


def msa_kernel(msa_ref, gain_ref, left_ref, right_ref, first_ref, second_ref, first, second, sems):
    seqs, cols, features = msa_ref.shape
    hidden = left_ref.shape[0]
    width = hidden * seqs
    chips, part, _ = second.shape
    left_rows = first.shape[1] - part
    pairs = width // hidden
    spread = ones_where(iota((hidden, width), 1) // seqs == iota((hidden, width), 0))
    right_copies = lax.dot_general(
        right_ref[...], spread, (((0,), (0,)), ((), ())), preferred_element_type=jnp.float32
    )
    right_lane = iota(right_copies.shape, 1) % seqs
    tiled = ones_where(iota((hidden, width), 1) % hidden == iota((hidden, width), 0))
    left_copies = lax.dot_general(
        left_ref[...], tiled, (((0,), (0,)), ((), ())), preferred_element_type=jnp.float32
    ).astype(jnp.bfloat16)
    own_lane = iota((cols, width), 1) // hidden == iota((cols, width), 0) // 2 % pairs
    place = (chips * left_rows, cols)
    target, source = iota(place, 0), iota(place, 1)
    same_pair = (target // left_rows == source // left_rows) & (
        target // seqs % 2 == source % 2
    )
    right = jnp.zeros((cols, width), jnp.float32)
    left = jnp.zeros((chips * left_rows, width), jnp.float32)
    for s in range(seqs):
        normed = standardize_features(msa_ref[s].astype(jnp.float32), gain_ref[...]).astype(
            jnp.bfloat16
        )
        right = right + jnp.dot(
            normed,
            jnp.where(right_lane == s, right_copies, 0.0).astype(jnp.bfloat16),
            preferred_element_type=jnp.float32,
        )
        products = jnp.dot(normed, left_copies, preferred_element_type=jnp.float32)
        left = left + jnp.dot(
            ones_where(same_pair & (target % seqs == s)),
            jnp.where(own_lane, products, 0.0).astype(jnp.bfloat16),
            preferred_element_type=jnp.float32,
        )
    right = right.astype(jnp.bfloat16)
    left = left.astype(jnp.bfloat16)
    for chip in range(chips):
        first[chip, :part, :] = right[:part]
        first[chip, part:, :] = left[chip * left_rows : (chip + 1) * left_rows]
        second[chip] = right[part:]
    copies = [
        pltpu.make_async_copy(
            block, send_ref.at[pl.ds(group * chips, chips)], sems.at[k, group]
        )
        for k, (block, send_ref) in enumerate(((first, first_ref), (second, second_ref)))
        for group in range(first_ref.shape[0] // chips)
    ]
    for copy in copies:
        copy.start()
    for copy in copies:
        copy.wait()


def whole(shape):
    return pl.BlockSpec(shape, lambda *_: (0,) * len(shape))


def msa_payload(msa, gain, left, right, groups, chips, left_rows):
    seqs, cols, features = msa.shape
    width = seqs * left.shape[1]
    operands = (msa, gain.reshape(1, features), left.T, right.T)
    return pl.pallas_call(
        msa_kernel,
        grid=(1,),
        in_specs=[whole(operand.shape) for operand in operands],
        out_specs=[pl.BlockSpec(memory_space=pl.ANY)] * 2,
        out_shape=[
            jax.ShapeDtypeStruct((groups * chips, count, width), jnp.bfloat16)
            for count in (cols // 2 + left_rows, cols // 2)
        ],
        scratch_shapes=[
            pltpu.VMEM((chips, cols // 2 + left_rows, width), jnp.bfloat16),
            pltpu.VMEM((chips, cols // 2, width), jnp.bfloat16),
            pltpu.SemaphoreType.DMA((2, groups)),
        ],
        compiler_params=pltpu.CompilerParams(vmem_limit_bytes=58 * MIB),
    )(*operands)


def opm_kernel(
    own, place_ref, gathered_ref, left_ref, weight_ref, out_ref, right_rows, left_block, left_rows, mixer, sems
):
    groups, cols, _ = right_rows.shape
    _, chips, _, width = gathered_ref.shape
    pairs, stacked, hidden = left_rows.shape
    seqs = width // hidden
    channels = weight_ref.shape[1] // hidden
    here = out_ref.shape[0] // 2
    copies = [
        pltpu.make_async_copy(
            gathered_ref.at[:, chip, pl.ds(0, cols), :],
            right_rows.at[:, :, pl.ds(chip * width, width)],
            sems.at[chip],
        )
        for chip in range(chips)
    ]
    left_copy = pltpu.make_async_copy(
        left_ref.at[place_ref[0], :, pl.ds(left_ref.shape[2] - 2 * seqs, 2 * seqs), :],
        left_block,
        sems.at[chips],
    )

    @pl.when(pl.program_id(0) == 0)
    def _():
        left_copy.start()
        for copy in copies:
            copy.start()
        left_copy.wait()
        half = place_ref[1] if own else 1 - place_ref[1]
        half = pl.multiple_of(half * (pairs * hidden), pairs * hidden)
        left = left_block[:, :, pl.ds(half, pairs * hidden)].reshape(stacked, pairs * hidden)
        for pair in range(pairs):
            left_rows[pair] = left[:, pair * hidden : (pair + 1) * hidden]

    step = 16 // seqs
    for pair in range(here):
        expanded = jnp.dot(
            left_rows[pl.program_id(0) * here + pair],
            weight_ref[...],
            preferred_element_type=jnp.float32,
        )
        for chip in range(chips):
            for row in range(2):
                start = (chip * 2 + row) * seqs
                column = (pair * 2 + row) * channels
                for d in range(0, hidden, step):
                    tile = jnp.concatenate(
                        [
                            expanded[start : start + seqs, k * channels : (k + 1) * channels]
                            for k in range(d, d + step)
                        ],
                        axis=0,
                    )
                    mixer[
                        chip * width + d * seqs : chip * width + (d + step) * seqs,
                        column : column + channels,
                    ] = tile.astype(jnp.bfloat16)

    @pl.when(pl.program_id(0) == 0)
    def _():
        for copy in copies:
            copy.wait()

    out = jnp.dot(
        right_rows[...].reshape(groups * cols, chips * width),
        mixer[...],
        preferred_element_type=jnp.float32,
    )
    for row in range(out_ref.shape[0]):
        out_ref[row] = out[:, row * channels : (row + 1) * channels].astype(out_ref.dtype)


def opm_rows(own, place, gathered, left, weight, cols, rows, step_rows=4):
    groups, chips, rows_sent, width = gathered.shape
    hidden = weight.shape[0]
    channels = weight.shape[1] // hidden
    seqs = width // hidden
    return pl.pallas_call(
        functools.partial(opm_kernel, own),
        grid=(rows // step_rows,),
        in_specs=[
            pl.BlockSpec(memory_space=pltpu.SMEM),
            pl.BlockSpec(memory_space=pl.ANY),
            pl.BlockSpec(memory_space=pl.ANY),
            whole(weight.shape),
        ],
        out_specs=pl.BlockSpec((step_rows, groups * cols, channels), lambda i: (i, 0, 0)),
        out_shape=jax.ShapeDtypeStruct((rows, groups * cols, channels), jnp.bfloat16),
        scratch_shapes=[
            pltpu.VMEM((groups, cols, chips * width), jnp.bfloat16),
            pltpu.VMEM((chips, 2 * seqs, width), jnp.bfloat16),
            pltpu.VMEM((rows // 2, chips * 2 * seqs, hidden), jnp.bfloat16),
            pltpu.VMEM((chips * width, step_rows * channels), jnp.bfloat16),
            pltpu.SemaphoreType.DMA((chips + 1,)),
        ],
        compiler_params=pltpu.CompilerParams(vmem_limit_bytes=24 * MIB),
        cost_estimate=pl.CostEstimate(
            flops=2 * rows * groups * cols * chips * width * channels,
            bytes_accessed=gathered.size * 2 + rows * groups * cols * channels * 2,
            transcendentals=0,
        ),
    )(place, gathered, left, weight)


def half_sigmoid(values):
    return 0.5 * jnp.tanh(0.5 * values) + 0.5


def pair_kernel(
    scale, pair_ref, own_ref, arrived_ref, gain_ref, *rest
):
    *weight_refs, updated_ref, normed_ref, send_ref, rows_buf, weight_buf = rest
    rows, cols, width = own_ref.shape
    channels = weight_refs[0].shape[1]

    @pl.when(pl.program_id(0) == 0)
    def _():
        for k, weight_ref in enumerate(weight_refs):
            weight_buf[k * channels : (k + 1) * channels, :] = weight_ref[...].T

    for row in range(rows):
        updated = (
            pair_ref[row].reshape(cols, width).astype(jnp.float32)
            + (own_ref[row].astype(jnp.float32) + arrived_ref[row].astype(jnp.float32)) * scale
        ).astype(jnp.bfloat16)
        updated_ref[row] = updated
        normed = standardize_features(updated.astype(jnp.float32), gain_ref[...]).astype(
            jnp.bfloat16
        )
        normed_ref[row] = normed
        products = lax.dot_general(
            weight_buf[...], normed, (((1,), (1,)), ((), ())), preferred_element_type=jnp.float32
        )
        for side in range(2):
            start = 2 * side * channels
            gated = products[start : start + channels] * half_sigmoid(
                products[start + channels : start + 2 * channels]
            )
            for lane in range(0, cols, 128):
                rows_buf[lane // 128, pl.ds(side * rows + row, channels, stride=2 * rows), :] = (
                    gated[:, lane : lane + 128]
                )
    for lane in range(0, cols, 128):
        send_ref[:, :, lane : lane + 128] = (
            rows_buf[lane // 128].reshape(channels, 2 * rows, 128).astype(jnp.bfloat16)
        )


def pair_operands(half, pair, own, arrived, gain, weights, scale):
    rows, length, width = own.shape
    groups = pair.shape[1]
    part = length // groups
    channels = weights[0].shape[1]
    cols = 256
    block = pl.BlockSpec((rows, cols, width), lambda i: (0, i, 0))
    return pl.pallas_call(
        functools.partial(pair_kernel, scale),
        grid=(length // cols,),
        in_specs=[
            pl.BlockSpec((rows, cols // part, part, width), lambda i: (0, i, half, 0)),
            block,
            block,
            pl.BlockSpec((1, width), lambda i: (0, 0)),
        ]
        + [whole(weight.shape) for weight in weights],
        out_specs=[
            block,
            block,
            pl.BlockSpec((channels, 2 * rows, cols), lambda i: (0, 0, i)),
        ],
        out_shape=[
            jax.ShapeDtypeStruct(own.shape, jnp.bfloat16),
            jax.ShapeDtypeStruct(own.shape, jnp.bfloat16),
            jax.ShapeDtypeStruct((channels, 2 * rows, length), jnp.bfloat16),
        ],
        scratch_shapes=[
            pltpu.VMEM((cols // 128, channels * 2 * rows, 128), jnp.float32),
            pltpu.VMEM((len(weights) * channels, width), jnp.bfloat16),
        ],
        compiler_params=pltpu.CompilerParams(vmem_limit_bytes=18 * MIB),
        cost_estimate=pl.CostEstimate(
            flops=8 * rows * length * width * channels,
            bytes_accessed=rows * length * width * 18,
            transcendentals=2 * rows * length * channels,
        ),
    )(pair, own, arrived, gain.reshape(1, width), *weights)


def result_kernel(mixed_ref, *refs):
    *halves, gain_ref, weight_ref, out_ref, rows_buf = refs
    channels, rows, cols = mixed_ref.shape
    for lane in range(0, cols, 128):
        values = mixed_ref[:, :, lane : lane + 128].astype(jnp.float32)
        center = values - jnp.mean(values, axis=0, keepdims=True)
        spread = jnp.mean(center * center, axis=0, keepdims=True)
        scaled = center * (1.0 / jnp.sqrt(spread + 1e-05))
        rows_buf[...] = scaled.reshape(channels * rows, 128)
        normed = jnp.concatenate(
            [rows_buf[pl.ds(row, channels, stride=rows), :] * gain_ref[...] for row in range(rows)],
            axis=1,
        ).astype(jnp.bfloat16)
        term = lax.dot_general(
            normed, weight_ref[...], (((0,), (0,)), ((), ())), preferred_element_type=jnp.float32
        ).reshape(rows, 128, -1)
        for half in range(2):
            updated_ref, gate_ref = halves[2 * half : 2 * half + 2]
            place = pl.ds(lane // 2, 64)
            out_ref[:, lane + 64 * half : lane + 64 * half + 64, :] = (
                updated_ref[:, place, :].astype(jnp.float32)
                + gate_ref[:, place, :].astype(jnp.float32)
                * term[:, 64 * half : 64 * half + 64]
            ).astype(jnp.bfloat16)


def result_rows(mixed, halves, gain, weight):
    channels, rows, length = mixed.shape
    width = weight.shape[1]
    cols = 256
    half_block = pl.BlockSpec((rows, cols // 2, width), lambda i: (0, i, 0))
    return pl.pallas_call(
        result_kernel,
        grid=(length // cols,),
        in_specs=[pl.BlockSpec((channels, rows, cols), lambda i: (0, 0, i))]
        + [half_block] * len(halves)
        + [whole((channels, 1)), whole(weight.shape)],
        out_specs=pl.BlockSpec((rows, cols, width), lambda i: (0, i, 0)),
        out_shape=jax.ShapeDtypeStruct((rows, length, width), jnp.bfloat16),
        scratch_shapes=[pltpu.VMEM((channels * rows, 128), jnp.float32)],
        compiler_params=pltpu.CompilerParams(vmem_limit_bytes=56 * MIB),
        cost_estimate=pl.CostEstimate(
            flops=2 * rows * length * width * channels,
            bytes_accessed=rows * length * width * 8,
            transcendentals=0,
        ),
    )(mixed, *halves, gain.reshape(channels, 1), weight)


def body(
    stacked_relatives_tensor,
    couple_embedding,
    relatives_rescaler,
    averaged_lhs_weights,
    averaged_rhs_weights,
    mean_final_linear,
    couple_scale_vector,
    first_linear_map,
    first_sigmoid_factor,
    second_linear_map,
    second_sigmoid_factor,
    final_sigmoid_factor,
    trio_scale_vector,
    trio_final_linear,
):
    groups, chips, cores = (lax.axis_size(name) for name in ALL)
    devices = groups * chips * cores
    seqs, cols, features = stacked_relatives_tensor.shape
    hidden = averaged_lhs_weights.shape[1]
    depth = seqs * chips * cores
    rows, length, pair_width = couple_embedding.shape

    payloads = msa_payload(
        stacked_relatives_tensor,
        relatives_rescaler,
        averaged_lhs_weights,
        averaged_rhs_weights,
        groups,
        chips,
        cores * rows,
    )
    part = cols // 2
    gathered = [
        lax.all_to_all(
            payload, ("dap", "chip"), split_axis=0, concat_axis=0, tiled=True
        ).reshape(groups, chips, *payload.shape[1:])
        for payload in payloads
    ]
    weight = mean_final_linear.reshape(hidden, hidden * pair_width)
    place = jnp.stack([lax.axis_index("dap"), lax.axis_index("core")])
    pair = couple_embedding.reshape(rows, groups, cols, pair_width)
    tri_weights = (
        first_linear_map, first_sigmoid_factor, second_linear_map, second_sigmoid_factor
    )
    halves, operands = [], []
    for half in range(2):
        other_part = opm_rows(False, place, gathered[half], gathered[0], weight, part, rows)
        arrived = lax.ppermute(other_part, "core", [(0, 1), (1, 0)])
        own_part = opm_rows(True, place, gathered[half], gathered[0], weight, part, rows)
        updated, pair_normed, send = pair_operands(
            half, pair, own_part, arrived, couple_scale_vector, tri_weights, 1.0 / depth
        )
        gate = jax.nn.sigmoid(
            jnp.dot(pair_normed, final_sigmoid_factor, preferred_element_type=jnp.float32)
        ).astype(jnp.bfloat16)
        halves += [updated, gate]
        operands.append(lax.all_to_all(send, ALL, split_axis=0, concat_axis=0, tiled=True))
    products = [
        functools.partial(
            lax.dot_general,
            operand[:, :rows].reshape(devices * rows, length // 2),
            operand[:, rows:].reshape(devices * rows, length // 2),
            (((1,), (1,)), ((), ())),
            preferred_element_type=jnp.float32,
        )
        for operand in operands
    ]
    first_half = lax.optimization_barrier(products[0]().astype(jnp.bfloat16))
    mixed = (first_half.astype(jnp.float32) + products[1]()).astype(jnp.bfloat16)
    mixed_back = lax.all_to_all(
        mixed.reshape(devices, rows, length), ALL, split_axis=0, concat_axis=0, tiled=True
    )
    return result_rows(mixed_back, halves, trio_scale_vector, trio_final_linear)


def solution(mesh):
    groups, lanes = mesh.shape["dap"], mesh.shape["bulk"]
    fine = Mesh(mesh.devices.reshape(groups, lanes // 2, 2), ALL)
    return jax.shard_map(
        body,
        mesh=fine,
        in_specs=(P(("chip", "core"), "dap", None), P(ALL, None, None)) + (P(),) * 12,
        out_specs=P(ALL, None, None),
        check_vma=False,
    )
```

```python
import functools

import jax
import jax.numpy as jnp
from jax import lax
from jax.experimental import pallas as pl
from jax.experimental.pallas import tpu as pltpu
from jax.sharding import Mesh, PartitionSpec as P

ALL = ("dap", "chip", "core")


def standardize_features(values, gain, axis=-1):
    center = values - jnp.mean(values, axis=axis, keepdims=True)
    spread = jnp.mean(center * center, axis=axis, keepdims=True)
    return center / jnp.sqrt(spread + 1e-05) * gain


MIB = 1024 * 1024


def ones_where(condition):
    return condition.astype(jnp.float32).astype(jnp.bfloat16)


def iota(shape, axis):
    return lax.broadcasted_iota(jnp.int32, shape, axis)


def msa_kernel(msa_ref, gain_ref, left_ref, right_ref, first_ref, second_ref, first, second, sems):
    seqs, cols, features = msa_ref.shape
    hidden = left_ref.shape[0]
    width = hidden * seqs
    chips, part, _ = second.shape
    left_rows = first.shape[1] - part
    pairs = width // hidden
    spread = ones_where(iota((hidden, width), 1) // seqs == iota((hidden, width), 0))
    right_copies = lax.dot_general(
        right_ref[...], spread, (((0,), (0,)), ((), ())), preferred_element_type=jnp.float32
    )
    right_lane = iota(right_copies.shape, 1) % seqs
    tiled = ones_where(iota((hidden, width), 1) % hidden == iota((hidden, width), 0))
    left_copies = lax.dot_general(
        left_ref[...], tiled, (((0,), (0,)), ((), ())), preferred_element_type=jnp.float32
    ).astype(jnp.bfloat16)
    own_lane = iota((cols, width), 1) // hidden == iota((cols, width), 0) // 2 % pairs
    place = (chips * left_rows, cols)
    target, source = iota(place, 0), iota(place, 1)
    same_pair = (target // left_rows == source // left_rows) & (
        target // seqs % 2 == source % 2
    )
    right = jnp.zeros((cols, width), jnp.float32)
    left = jnp.zeros((chips * left_rows, width), jnp.float32)
    for s in range(seqs):
        normed = standardize_features(msa_ref[s].astype(jnp.float32), gain_ref[...]).astype(
            jnp.bfloat16
        )
        right = right + jnp.dot(
            normed,
            jnp.where(right_lane == s, right_copies, 0.0).astype(jnp.bfloat16),
            preferred_element_type=jnp.float32,
        )
        products = jnp.dot(normed, left_copies, preferred_element_type=jnp.float32)
        left = left + jnp.dot(
            ones_where(same_pair & (target % seqs == s)),
            jnp.where(own_lane, products, 0.0).astype(jnp.bfloat16),
            preferred_element_type=jnp.float32,
        )
    right = right.astype(jnp.bfloat16)
    left = left.astype(jnp.bfloat16)
    for chip in range(chips):
        first[chip, :part, :] = right[:part]
        first[chip, part:, :] = left[chip * left_rows : (chip + 1) * left_rows]
        second[chip] = right[part:]
    copies = [
        pltpu.make_async_copy(
            block, send_ref.at[pl.ds(group * chips, chips)], sems.at[k, group]
        )
        for k, (block, send_ref) in enumerate(((first, first_ref), (second, second_ref)))
        for group in range(first_ref.shape[0] // chips)
    ]
    for copy in copies:
        copy.start()
    for copy in copies:
        copy.wait()


def whole(shape):
    return pl.BlockSpec(shape, lambda *_: (0,) * len(shape))


def msa_payload(msa, gain, left, right, groups, chips, left_rows):
    seqs, cols, features = msa.shape
    width = seqs * left.shape[1]
    operands = (msa, gain.reshape(1, features), left.T, right.T)
    return pl.pallas_call(
        msa_kernel,
        grid=(1,),
        in_specs=[whole(operand.shape) for operand in operands],
        out_specs=[pl.BlockSpec(memory_space=pl.ANY)] * 2,
        out_shape=[
            jax.ShapeDtypeStruct((groups * chips, count, width), jnp.bfloat16)
            for count in (cols // 2 + left_rows, cols // 2)
        ],
        scratch_shapes=[
            pltpu.VMEM((chips, cols // 2 + left_rows, width), jnp.bfloat16),
            pltpu.VMEM((chips, cols // 2, width), jnp.bfloat16),
            pltpu.SemaphoreType.DMA((2, groups)),
        ],
        compiler_params=pltpu.CompilerParams(vmem_limit_bytes=58 * MIB),
    )(*operands)


def opm_kernel(
    own, place_ref, gathered_ref, left_ref, weight_ref, out_ref, right_rows, left_block, left_rows, mixer, sems
):
    groups, cols, _ = right_rows.shape
    _, chips, _, width = gathered_ref.shape
    pairs, stacked, hidden = left_rows.shape
    seqs = width // hidden
    channels = weight_ref.shape[1] // hidden
    here = out_ref.shape[0] // 2
    copies = [
        pltpu.make_async_copy(
            gathered_ref.at[:, chip, pl.ds(0, cols), :],
            right_rows.at[:, :, pl.ds(chip * width, width)],
            sems.at[chip],
        )
        for chip in range(chips)
    ]
    left_copy = pltpu.make_async_copy(
        left_ref.at[place_ref[0], :, pl.ds(left_ref.shape[2] - 2 * seqs, 2 * seqs), :],
        left_block,
        sems.at[chips],
    )

    @pl.when(pl.program_id(0) == 0)
    def _():
        left_copy.start()
        for copy in copies:
            copy.start()
        left_copy.wait()
        half = place_ref[1] if own else 1 - place_ref[1]
        half = pl.multiple_of(half * (pairs * hidden), pairs * hidden)
        left = left_block[:, :, pl.ds(half, pairs * hidden)].reshape(stacked, pairs * hidden)
        for pair in range(pairs):
            left_rows[pair] = left[:, pair * hidden : (pair + 1) * hidden]

    step = 16 // seqs
    for pair in range(here):
        expanded = jnp.dot(
            left_rows[pl.program_id(0) * here + pair],
            weight_ref[...],
            preferred_element_type=jnp.float32,
        )
        for chip in range(chips):
            for row in range(2):
                start = (chip * 2 + row) * seqs
                column = (pair * 2 + row) * channels
                for d in range(0, hidden, step):
                    tile = jnp.concatenate(
                        [
                            expanded[start : start + seqs, k * channels : (k + 1) * channels]
                            for k in range(d, d + step)
                        ],
                        axis=0,
                    )
                    mixer[
                        chip * width + d * seqs : chip * width + (d + step) * seqs,
                        column : column + channels,
                    ] = tile.astype(jnp.bfloat16)

    @pl.when(pl.program_id(0) == 0)
    def _():
        for copy in copies:
            copy.wait()

    out = jnp.dot(
        right_rows[...].reshape(groups * cols, chips * width),
        mixer[...],
        preferred_element_type=jnp.float32,
    )
    for row in range(out_ref.shape[0]):
        out_ref[row] = out[:, row * channels : (row + 1) * channels].astype(out_ref.dtype)


def opm_rows(own, place, gathered, left, weight, cols, rows, step_rows=4):
    groups, chips, rows_sent, width = gathered.shape
    hidden = weight.shape[0]
    channels = weight.shape[1] // hidden
    seqs = width // hidden
    return pl.pallas_call(
        functools.partial(opm_kernel, own),
        grid=(rows // step_rows,),
        in_specs=[
            pl.BlockSpec(memory_space=pltpu.SMEM),
            pl.BlockSpec(memory_space=pl.ANY),
            pl.BlockSpec(memory_space=pl.ANY),
            whole(weight.shape),
        ],
        out_specs=pl.BlockSpec((step_rows, groups * cols, channels), lambda i: (i, 0, 0)),
        out_shape=jax.ShapeDtypeStruct((rows, groups * cols, channels), jnp.bfloat16),
        scratch_shapes=[
            pltpu.VMEM((groups, cols, chips * width), jnp.bfloat16),
            pltpu.VMEM((chips, 2 * seqs, width), jnp.bfloat16),
            pltpu.VMEM((rows // 2, chips * 2 * seqs, hidden), jnp.bfloat16),
            pltpu.VMEM((chips * width, step_rows * channels), jnp.bfloat16),
            pltpu.SemaphoreType.DMA((chips + 1,)),
        ],
        compiler_params=pltpu.CompilerParams(vmem_limit_bytes=24 * MIB),
        cost_estimate=pl.CostEstimate(
            flops=2 * rows * groups * cols * chips * width * channels,
            bytes_accessed=gathered.size * 2 + rows * groups * cols * channels * 2,
            transcendentals=0,
        ),
    )(place, gathered, left, weight)


def half_sigmoid(values):
    return 0.5 * jnp.tanh(0.5 * values) + 0.5


def pair_kernel(
    scale, pair_ref, own_ref, arrived_ref, gain_ref, *rest
):
    *weight_refs, updated_ref, normed_ref, send_ref, rows_buf, weight_buf = rest
    rows, cols, width = own_ref.shape
    channels = weight_refs[0].shape[1]

    @pl.when(pl.program_id(0) == 0)
    def _():
        for k, weight_ref in enumerate(weight_refs):
            weight_buf[k * channels : (k + 1) * channels, :] = weight_ref[...].T

    for row in range(rows):
        updated = (
            pair_ref[row].reshape(cols, width).astype(jnp.float32)
            + (own_ref[row].astype(jnp.float32) + arrived_ref[row].astype(jnp.float32)) * scale
        ).astype(jnp.bfloat16)
        updated_ref[row] = updated
        normed = standardize_features(updated.astype(jnp.float32), gain_ref[...]).astype(
            jnp.bfloat16
        )
        normed_ref[row] = normed
        products = lax.dot_general(
            weight_buf[...], normed, (((1,), (1,)), ((), ())), preferred_element_type=jnp.float32
        )
        for side in range(2):
            start = 2 * side * channels
            gated = products[start : start + channels] * half_sigmoid(
                products[start + channels : start + 2 * channels]
            )
            for lane in range(0, cols, 128):
                rows_buf[lane // 128, pl.ds(side * rows + row, channels, stride=2 * rows), :] = (
                    gated[:, lane : lane + 128]
                )
    for lane in range(0, cols, 128):
        send_ref[:, :, lane : lane + 128] = (
            rows_buf[lane // 128, : channels * 2 * rows, :]
            .reshape(channels, 2 * rows, 128)
            .astype(jnp.bfloat16)
        )


def pair_operands(half, pair, own, arrived, gain, weights, scale):
    rows, length, width = own.shape
    groups = pair.shape[1]
    part = length // groups
    channels = weights[0].shape[1]
    cols = 256
    block = pl.BlockSpec((rows, cols, width), lambda i: (0, i, 0))
    return pl.pallas_call(
        functools.partial(pair_kernel, scale),
        grid=(length // cols,),
        in_specs=[
            pl.BlockSpec((rows, cols // part, part, width), lambda i: (0, i, half, 0)),
            block,
            block,
            pl.BlockSpec((1, width), lambda i: (0, 0)),
        ]
        + [whole(weight.shape) for weight in weights],
        out_specs=[
            block,
            block,
            pl.BlockSpec((channels, 2 * rows, cols), lambda i: (0, 0, i)),
        ],
        out_shape=[
            jax.ShapeDtypeStruct(own.shape, jnp.bfloat16),
            jax.ShapeDtypeStruct(own.shape, jnp.bfloat16),
            jax.ShapeDtypeStruct((channels, 2 * rows, length), jnp.bfloat16),
        ],
        scratch_shapes=[
            pltpu.VMEM((cols // 128, (channels + 1) * 2 * rows, 128), jnp.float32),
            pltpu.VMEM((len(weights) * channels, width), jnp.bfloat16),
        ],
        compiler_params=pltpu.CompilerParams(vmem_limit_bytes=18 * MIB),
        cost_estimate=pl.CostEstimate(
            flops=8 * rows * length * width * channels,
            bytes_accessed=rows * length * width * 18,
            transcendentals=2 * rows * length * channels,
        ),
    )(pair, own, arrived, gain.reshape(1, width), *weights)


def result_kernel(mixed_ref, *refs):
    *halves, gain_ref, weight_ref, out_ref, rows_buf = refs
    channels, rows, cols = mixed_ref.shape
    for lane in range(0, cols, 128):
        values = mixed_ref[:, :, lane : lane + 128].astype(jnp.float32)
        center = values - jnp.mean(values, axis=0, keepdims=True)
        spread = jnp.mean(center * center, axis=0, keepdims=True)
        scaled = center * (1.0 / jnp.sqrt(spread + 1e-05))
        rows_buf[: channels * rows, :] = scaled.reshape(channels * rows, 128)
        normed = jnp.concatenate(
            [rows_buf[pl.ds(row, channels, stride=rows), :] * gain_ref[...] for row in range(rows)],
            axis=1,
        ).astype(jnp.bfloat16)
        term = lax.dot_general(
            normed, weight_ref[...], (((0,), (0,)), ((), ())), preferred_element_type=jnp.float32
        ).reshape(rows, 128, -1)
        for half in range(2):
            updated_ref, gate_ref = halves[2 * half : 2 * half + 2]
            place = pl.ds(lane // 2, 64)
            out_ref[:, lane + 64 * half : lane + 64 * half + 64, :] = (
                updated_ref[:, place, :].astype(jnp.float32)
                + gate_ref[:, place, :].astype(jnp.float32)
                * term[:, 64 * half : 64 * half + 64]
            ).astype(jnp.bfloat16)


def result_rows(mixed, halves, gain, weight):
    channels, rows, length = mixed.shape
    width = weight.shape[1]
    cols = 256
    half_block = pl.BlockSpec((rows, cols // 2, width), lambda i: (0, i, 0))
    return pl.pallas_call(
        result_kernel,
        grid=(length // cols,),
        in_specs=[pl.BlockSpec((channels, rows, cols), lambda i: (0, 0, i))]
        + [half_block] * len(halves)
        + [whole((channels, 1)), whole(weight.shape)],
        out_specs=pl.BlockSpec((rows, cols, width), lambda i: (0, i, 0)),
        out_shape=jax.ShapeDtypeStruct((rows, length, width), jnp.bfloat16),
        scratch_shapes=[pltpu.VMEM(((channels + 1) * rows, 128), jnp.float32)],
        compiler_params=pltpu.CompilerParams(vmem_limit_bytes=56 * MIB),
        cost_estimate=pl.CostEstimate(
            flops=2 * rows * length * width * channels,
            bytes_accessed=rows * length * width * 8,
            transcendentals=0,
        ),
    )(mixed, *halves, gain.reshape(channels, 1), weight)


def body(
    stacked_relatives_tensor,
    couple_embedding,
    relatives_rescaler,
    averaged_lhs_weights,
    averaged_rhs_weights,
    mean_final_linear,
    couple_scale_vector,
    first_linear_map,
    first_sigmoid_factor,
    second_linear_map,
    second_sigmoid_factor,
    final_sigmoid_factor,
    trio_scale_vector,
    trio_final_linear,
):
    groups, chips, cores = (lax.axis_size(name) for name in ALL)
    devices = groups * chips * cores
    seqs, cols, features = stacked_relatives_tensor.shape
    hidden = averaged_lhs_weights.shape[1]
    depth = seqs * chips * cores
    rows, length, pair_width = couple_embedding.shape

    payloads = msa_payload(
        stacked_relatives_tensor,
        relatives_rescaler,
        averaged_lhs_weights,
        averaged_rhs_weights,
        groups,
        chips,
        cores * rows,
    )
    part = cols // 2
    gathered = [
        lax.all_to_all(
            payload, ("dap", "chip"), split_axis=0, concat_axis=0, tiled=True
        ).reshape(groups, chips, *payload.shape[1:])
        for payload in payloads
    ]
    weight = mean_final_linear.reshape(hidden, hidden * pair_width)
    place = jnp.stack([lax.axis_index("dap"), lax.axis_index("core")])
    pair = couple_embedding.reshape(rows, groups, cols, pair_width)
    tri_weights = (
        first_linear_map, first_sigmoid_factor, second_linear_map, second_sigmoid_factor
    )
    halves, operands = [], []
    for half in range(2):
        other_part = opm_rows(False, place, gathered[half], gathered[0], weight, part, rows)
        arrived = lax.ppermute(other_part, "core", [(0, 1), (1, 0)])
        own_part = opm_rows(True, place, gathered[half], gathered[0], weight, part, rows)
        updated, pair_normed, send = pair_operands(
            half, pair, own_part, arrived, couple_scale_vector, tri_weights, 1.0 / depth
        )
        gate = jax.nn.sigmoid(
            jnp.dot(pair_normed, final_sigmoid_factor, preferred_element_type=jnp.float32)
        ).astype(jnp.bfloat16)
        halves += [updated, gate]
        operands.append(lax.all_to_all(send, ALL, split_axis=0, concat_axis=0, tiled=True))
    products = [
        functools.partial(
            lax.dot_general,
            operand[:, :rows].reshape(devices * rows, length // 2),
            operand[:, rows:].reshape(devices * rows, length // 2),
            (((1,), (1,)), ((), ())),
            preferred_element_type=jnp.float32,
        )
        for operand in operands
    ]
    first_half = lax.optimization_barrier(products[0]().astype(jnp.bfloat16))
    mixed = (first_half.astype(jnp.float32) + products[1]()).astype(jnp.bfloat16)
    mixed_back = lax.all_to_all(
        mixed.reshape(devices, rows, length), ALL, split_axis=0, concat_axis=0, tiled=True
    )
    return result_rows(mixed_back, halves, trio_scale_vector, trio_final_linear)


def solution(mesh):
    groups, lanes = mesh.shape["dap"], mesh.shape["bulk"]
    fine = Mesh(mesh.devices.reshape(groups, lanes // 2, 2), ALL)
    return jax.shard_map(
        body,
        mesh=fine,
        in_specs=(P(("chip", "core"), "dap", None), P(ALL, None, None)) + (P(),) * 12,
        out_specs=P(ALL, None, None),
        check_vma=False,
    )
```

```python
import functools

import jax
import jax.numpy as jnp
from jax import lax
from jax.experimental import pallas as pl
from jax.experimental.pallas import tpu as pltpu
from jax.sharding import Mesh, PartitionSpec as P

ALL = ("dap", "chip", "core")


def standardize_features(values, gain, axis=-1):
    center = values - jnp.mean(values, axis=axis, keepdims=True)
    spread = jnp.mean(center * center, axis=axis, keepdims=True)
    return center / jnp.sqrt(spread + 1e-05) * gain


MIB = 1024 * 1024


def ones_where(condition):
    return condition.astype(jnp.float32).astype(jnp.bfloat16)


def iota(shape, axis):
    return lax.broadcasted_iota(jnp.int32, shape, axis)


def msa_kernel(msa_ref, gain_ref, left_ref, right_ref, first_ref, second_ref, first, second, sems):
    seqs, cols, features = msa_ref.shape
    hidden = left_ref.shape[0]
    width = hidden * seqs
    chips, part, _ = second.shape
    left_rows = first.shape[1] - part
    pairs = width // hidden
    spread = ones_where(iota((hidden, width), 1) // seqs == iota((hidden, width), 0))
    right_copies = lax.dot_general(
        right_ref[...], spread, (((0,), (0,)), ((), ())), preferred_element_type=jnp.float32
    )
    right_lane = iota(right_copies.shape, 1) % seqs
    tiled = ones_where(iota((hidden, width), 1) % hidden == iota((hidden, width), 0))
    left_copies = lax.dot_general(
        left_ref[...], tiled, (((0,), (0,)), ((), ())), preferred_element_type=jnp.float32
    ).astype(jnp.bfloat16)
    own_lane = iota((cols, width), 1) // hidden == iota((cols, width), 0) // 2 % pairs
    place = (chips * left_rows, cols)
    target, source = iota(place, 0), iota(place, 1)
    same_pair = (target // left_rows == source // left_rows) & (
        target // seqs % 2 == source % 2
    )
    def replicated(block, send_ref, k):
        return [
            pltpu.make_async_copy(
                block, send_ref.at[pl.ds(group * chips, chips)], sems.at[k, group]
            )
            for group in range(send_ref.shape[0] // chips)
        ]

    right = jnp.zeros((cols, width), jnp.float32)
    normed = []
    for s in range(seqs):
        normed.append(
            standardize_features(msa_ref[s].astype(jnp.float32), gain_ref[...]).astype(
                jnp.bfloat16
            )
        )
        right = right + jnp.dot(
            normed[s],
            jnp.where(right_lane == s, right_copies, 0.0).astype(jnp.bfloat16),
            preferred_element_type=jnp.float32,
        )
    right = right.astype(jnp.bfloat16)
    for chip in range(chips):
        second[chip] = right[part:]
    second_copies = replicated(second, second_ref, 1)
    for copy in second_copies:
        copy.start()
    left = jnp.zeros((chips * left_rows, width), jnp.float32)
    for s in range(seqs):
        products = jnp.dot(normed[s], left_copies, preferred_element_type=jnp.float32)
        left = left + jnp.dot(
            ones_where(same_pair & (target % seqs == s)),
            jnp.where(own_lane, products, 0.0).astype(jnp.bfloat16),
            preferred_element_type=jnp.float32,
        )
    left = left.astype(jnp.bfloat16)
    for chip in range(chips):
        first[chip, :part, :] = right[:part]
        first[chip, part:, :] = left[chip * left_rows : (chip + 1) * left_rows]
    first_copies = replicated(first, first_ref, 0)
    for copy in first_copies:
        copy.start()
    for copy in second_copies + first_copies:
        copy.wait()


def whole(shape):
    return pl.BlockSpec(shape, lambda *_: (0,) * len(shape))


def msa_payload(msa, gain, left, right, groups, chips, left_rows):
    seqs, cols, features = msa.shape
    width = seqs * left.shape[1]
    operands = (msa, gain.reshape(1, features), left.T, right.T)
    return pl.pallas_call(
        msa_kernel,
        grid=(1,),
        in_specs=[whole(operand.shape) for operand in operands],
        out_specs=[pl.BlockSpec(memory_space=pl.ANY)] * 2,
        out_shape=[
            jax.ShapeDtypeStruct((groups * chips, count, width), jnp.bfloat16)
            for count in (cols // 2 + left_rows, cols // 2)
        ],
        scratch_shapes=[
            pltpu.VMEM((chips, cols // 2 + left_rows, width), jnp.bfloat16),
            pltpu.VMEM((chips, cols // 2, width), jnp.bfloat16),
            pltpu.SemaphoreType.DMA((2, groups)),
        ],
        compiler_params=pltpu.CompilerParams(vmem_limit_bytes=58 * MIB),
    )(*operands)


def opm_kernel(
    own, place_ref, gathered_ref, left_ref, weight_ref, out_ref, right_rows, left_block, left_rows, mixer, sems
):
    groups, cols, _ = right_rows.shape
    _, chips, _, width = gathered_ref.shape
    pairs, stacked, hidden = left_rows.shape
    seqs = width // hidden
    channels = weight_ref.shape[1] // hidden
    here = out_ref.shape[0] // 2
    copies = [
        pltpu.make_async_copy(
            gathered_ref.at[:, chip, pl.ds(0, cols), :],
            right_rows.at[:, :, pl.ds(chip * width, width)],
            sems.at[chip],
        )
        for chip in range(chips)
    ]
    left_copy = pltpu.make_async_copy(
        left_ref.at[place_ref[0], :, pl.ds(left_ref.shape[2] - 2 * seqs, 2 * seqs), :],
        left_block,
        sems.at[chips],
    )

    @pl.when(pl.program_id(0) == 0)
    def _():
        left_copy.start()
        for copy in copies:
            copy.start()
        left_copy.wait()
        half = place_ref[1] if own else 1 - place_ref[1]
        half = pl.multiple_of(half * (pairs * hidden), pairs * hidden)
        left = left_block[:, :, pl.ds(half, pairs * hidden)].reshape(stacked, pairs * hidden)
        for pair in range(pairs):
            left_rows[pair] = left[:, pair * hidden : (pair + 1) * hidden]

    step = 16 // seqs
    for pair in range(here):
        expanded = jnp.dot(
            left_rows[pl.program_id(0) * here + pair],
            weight_ref[...],
            preferred_element_type=jnp.float32,
        )
        for chip in range(chips):
            for row in range(2):
                start = (chip * 2 + row) * seqs
                column = (pair * 2 + row) * channels
                for d in range(0, hidden, step):
                    tile = jnp.concatenate(
                        [
                            expanded[start : start + seqs, k * channels : (k + 1) * channels]
                            for k in range(d, d + step)
                        ],
                        axis=0,
                    )
                    mixer[
                        chip * width + d * seqs : chip * width + (d + step) * seqs,
                        column : column + channels,
                    ] = tile.astype(jnp.bfloat16)

    @pl.when(pl.program_id(0) == 0)
    def _():
        for copy in copies:
            copy.wait()

    out = jnp.dot(
        right_rows[...].reshape(groups * cols, chips * width),
        mixer[...],
        preferred_element_type=jnp.float32,
    )
    for row in range(out_ref.shape[0]):
        out_ref[row] = out[:, row * channels : (row + 1) * channels].astype(out_ref.dtype)


def opm_rows(own, place, gathered, left, weight, cols, rows, step_rows=4):
    groups, chips, rows_sent, width = gathered.shape
    hidden = weight.shape[0]
    channels = weight.shape[1] // hidden
    seqs = width // hidden
    return pl.pallas_call(
        functools.partial(opm_kernel, own),
        grid=(rows // step_rows,),
        in_specs=[
            pl.BlockSpec(memory_space=pltpu.SMEM),
            pl.BlockSpec(memory_space=pl.ANY),
            pl.BlockSpec(memory_space=pl.ANY),
            whole(weight.shape),
        ],
        out_specs=pl.BlockSpec((step_rows, groups * cols, channels), lambda i: (i, 0, 0)),
        out_shape=jax.ShapeDtypeStruct((rows, groups * cols, channels), jnp.bfloat16),
        scratch_shapes=[
            pltpu.VMEM((groups, cols, chips * width), jnp.bfloat16),
            pltpu.VMEM((chips, 2 * seqs, width), jnp.bfloat16),
            pltpu.VMEM((rows // 2, chips * 2 * seqs, hidden), jnp.bfloat16),
            pltpu.VMEM((chips * width, step_rows * channels), jnp.bfloat16),
            pltpu.SemaphoreType.DMA((chips + 1,)),
        ],
        compiler_params=pltpu.CompilerParams(vmem_limit_bytes=24 * MIB),
        cost_estimate=pl.CostEstimate(
            flops=2 * rows * groups * cols * chips * width * channels,
            bytes_accessed=gathered.size * 2 + rows * groups * cols * channels * 2,
            transcendentals=0,
        ),
    )(place, gathered, left, weight)


def half_sigmoid(values):
    return 0.5 * jnp.tanh(0.5 * values) + 0.5


def pair_kernel(
    scale, pair_ref, own_ref, arrived_ref, gain_ref, *rest
):
    *weight_refs, updated_ref, normed_ref, send_ref, rows_buf, weight_buf = rest
    rows, cols, width = own_ref.shape
    channels = weight_refs[0].shape[1]

    @pl.when(pl.program_id(0) == 0)
    def _():
        for k, weight_ref in enumerate(weight_refs):
            weight_buf[k * channels : (k + 1) * channels, :] = weight_ref[...].T

    for row in range(rows):
        updated = (
            pair_ref[row].reshape(cols, width).astype(jnp.float32)
            + (own_ref[row].astype(jnp.float32) + arrived_ref[row].astype(jnp.float32)) * scale
        ).astype(jnp.bfloat16)
        updated_ref[row] = updated
        normed = standardize_features(updated.astype(jnp.float32), gain_ref[...]).astype(
            jnp.bfloat16
        )
        normed_ref[row] = normed
        products = lax.dot_general(
            weight_buf[...], normed, (((1,), (1,)), ((), ())), preferred_element_type=jnp.float32
        )
        for side in range(2):
            start = 2 * side * channels
            gated = products[start : start + channels] * half_sigmoid(
                products[start + channels : start + 2 * channels]
            )
            for lane in range(0, cols, 128):
                rows_buf[lane // 128, pl.ds(side * rows + row, channels, stride=2 * rows), :] = (
                    gated[:, lane : lane + 128]
                )
    for lane in range(0, cols, 128):
        send_ref[:, :, lane : lane + 128] = (
            rows_buf[lane // 128, : channels * 2 * rows, :]
            .reshape(channels, 2 * rows, 128)
            .astype(jnp.bfloat16)
        )


def pair_operands(half, pair, own, arrived, gain, weights, scale):
    rows, length, width = own.shape
    groups = pair.shape[1]
    part = length // groups
    channels = weights[0].shape[1]
    cols = 256
    block = pl.BlockSpec((rows, cols, width), lambda i: (0, i, 0))
    return pl.pallas_call(
        functools.partial(pair_kernel, scale),
        grid=(length // cols,),
        in_specs=[
            pl.BlockSpec((rows, cols // part, part, width), lambda i: (0, i, half, 0)),
            block,
            block,
            pl.BlockSpec((1, width), lambda i: (0, 0)),
        ]
        + [whole(weight.shape) for weight in weights],
        out_specs=[
            block,
            block,
            pl.BlockSpec((channels, 2 * rows, cols), lambda i: (0, 0, i)),
        ],
        out_shape=[
            jax.ShapeDtypeStruct(own.shape, jnp.bfloat16),
            jax.ShapeDtypeStruct(own.shape, jnp.bfloat16),
            jax.ShapeDtypeStruct((channels, 2 * rows, length), jnp.bfloat16),
        ],
        scratch_shapes=[
            pltpu.VMEM((cols // 128, (channels + 1) * 2 * rows, 128), jnp.float32),
            pltpu.VMEM((len(weights) * channels, width), jnp.bfloat16),
        ],
        compiler_params=pltpu.CompilerParams(vmem_limit_bytes=18 * MIB),
        cost_estimate=pl.CostEstimate(
            flops=8 * rows * length * width * channels,
            bytes_accessed=rows * length * width * 18,
            transcendentals=2 * rows * length * channels,
        ),
    )(pair, own, arrived, gain.reshape(1, width), *weights)


def result_kernel(mixed_ref, *refs):
    *halves, gain_ref, weight_ref, out_ref, rows_buf = refs
    channels, rows, cols = mixed_ref.shape
    for lane in range(0, cols, 128):
        values = mixed_ref[:, :, lane : lane + 128].astype(jnp.float32)
        center = values - jnp.mean(values, axis=0, keepdims=True)
        spread = jnp.mean(center * center, axis=0, keepdims=True)
        scaled = center * (1.0 / jnp.sqrt(spread + 1e-05))
        rows_buf[: channels * rows, :] = scaled.reshape(channels * rows, 128)
        normed = jnp.concatenate(
            [rows_buf[pl.ds(row, channels, stride=rows), :] * gain_ref[...] for row in range(rows)],
            axis=1,
        ).astype(jnp.bfloat16)
        term = lax.dot_general(
            normed, weight_ref[...], (((0,), (0,)), ((), ())), preferred_element_type=jnp.float32
        ).reshape(rows, 128, -1)
        for half in range(2):
            updated_ref, gate_ref = halves[2 * half : 2 * half + 2]
            place = pl.ds(lane // 2, 64)
            out_ref[:, lane + 64 * half : lane + 64 * half + 64, :] = (
                updated_ref[:, place, :].astype(jnp.float32)
                + gate_ref[:, place, :].astype(jnp.float32)
                * term[:, 64 * half : 64 * half + 64]
            ).astype(jnp.bfloat16)


def result_rows(mixed, halves, gain, weight):
    channels, rows, length = mixed.shape
    width = weight.shape[1]
    cols = 256
    half_block = pl.BlockSpec((rows, cols // 2, width), lambda i: (0, i, 0))
    return pl.pallas_call(
        result_kernel,
        grid=(length // cols,),
        in_specs=[pl.BlockSpec((channels, rows, cols), lambda i: (0, 0, i))]
        + [half_block] * len(halves)
        + [whole((channels, 1)), whole(weight.shape)],
        out_specs=pl.BlockSpec((rows, cols, width), lambda i: (0, i, 0)),
        out_shape=jax.ShapeDtypeStruct((rows, length, width), jnp.bfloat16),
        scratch_shapes=[pltpu.VMEM(((channels + 1) * rows, 128), jnp.float32)],
        compiler_params=pltpu.CompilerParams(vmem_limit_bytes=56 * MIB),
        cost_estimate=pl.CostEstimate(
            flops=2 * rows * length * width * channels,
            bytes_accessed=rows * length * width * 8,
            transcendentals=0,
        ),
    )(mixed, *halves, gain.reshape(channels, 1), weight)


def body(
    stacked_relatives_tensor,
    couple_embedding,
    relatives_rescaler,
    averaged_lhs_weights,
    averaged_rhs_weights,
    mean_final_linear,
    couple_scale_vector,
    first_linear_map,
    first_sigmoid_factor,
    second_linear_map,
    second_sigmoid_factor,
    final_sigmoid_factor,
    trio_scale_vector,
    trio_final_linear,
):
    groups, chips, cores = (lax.axis_size(name) for name in ALL)
    devices = groups * chips * cores
    seqs, cols, features = stacked_relatives_tensor.shape
    hidden = averaged_lhs_weights.shape[1]
    depth = seqs * chips * cores
    rows, length, pair_width = couple_embedding.shape

    payloads = msa_payload(
        stacked_relatives_tensor,
        relatives_rescaler,
        averaged_lhs_weights,
        averaged_rhs_weights,
        groups,
        chips,
        cores * rows,
    )
    part = cols // 2
    gathered = [
        lax.all_to_all(
            payload, ("dap", "chip"), split_axis=0, concat_axis=0, tiled=True
        ).reshape(groups, chips, *payload.shape[1:])
        for payload in payloads
    ]
    weight = mean_final_linear.reshape(hidden, hidden * pair_width)
    place = jnp.stack([lax.axis_index("dap"), lax.axis_index("core")])
    pair = couple_embedding.reshape(rows, groups, cols, pair_width)
    tri_weights = (
        first_linear_map, first_sigmoid_factor, second_linear_map, second_sigmoid_factor
    )
    halves, operands = [], []
    for half in range(2):
        other_part = opm_rows(False, place, gathered[half], gathered[0], weight, part, rows)
        arrived = lax.ppermute(other_part, "core", [(0, 1), (1, 0)])
        own_part = opm_rows(True, place, gathered[half], gathered[0], weight, part, rows)
        updated, pair_normed, send = pair_operands(
            half, pair, own_part, arrived, couple_scale_vector, tri_weights, 1.0 / depth
        )
        gate = jax.nn.sigmoid(
            jnp.dot(pair_normed, final_sigmoid_factor, preferred_element_type=jnp.float32)
        ).astype(jnp.bfloat16)
        halves += [updated, gate]
        operands.append(lax.all_to_all(send, ALL, split_axis=0, concat_axis=0, tiled=True))
    products = [
        functools.partial(
            lax.dot_general,
            operand[:, :rows].reshape(devices * rows, length // 2),
            operand[:, rows:].reshape(devices * rows, length // 2),
            (((1,), (1,)), ((), ())),
            preferred_element_type=jnp.float32,
        )
        for operand in operands
    ]
    first_half = lax.optimization_barrier(products[0]().astype(jnp.bfloat16))
    mixed = (first_half.astype(jnp.float32) + products[1]()).astype(jnp.bfloat16)
    mixed_back = lax.all_to_all(
        mixed.reshape(devices, rows, length), ALL, split_axis=0, concat_axis=0, tiled=True
    )
    return result_rows(mixed_back, halves, trio_scale_vector, trio_final_linear)


def solution(mesh):
    groups, lanes = mesh.shape["dap"], mesh.shape["bulk"]
    fine = Mesh(mesh.devices.reshape(groups, lanes // 2, 2), ALL)
    return jax.shard_map(
        body,
        mesh=fine,
        in_specs=(P(("chip", "core"), "dap", None), P(ALL, None, None)) + (P(),) * 12,
        out_specs=P(ALL, None, None),
        check_vma=False,
    )
```

```python
import functools

import jax
import jax.numpy as jnp
from jax import lax
from jax.experimental import pallas as pl
from jax.experimental.pallas import tpu as pltpu
from jax.sharding import Mesh, PartitionSpec as P

ALL = ("dap", "chip", "core")


def standardize_features(values, gain, axis=-1):
    center = values - jnp.mean(values, axis=axis, keepdims=True)
    spread = jnp.mean(center * center, axis=axis, keepdims=True)
    return center / jnp.sqrt(spread + 1e-05) * gain


MIB = 1024 * 1024


def ones_where(condition):
    return condition.astype(jnp.float32).astype(jnp.bfloat16)


def iota(shape, axis):
    return lax.broadcasted_iota(jnp.int32, shape, axis)


def msa_kernel(msa_ref, gain_ref, left_ref, right_ref, first_ref, second_ref, first, second, sems):
    seqs, cols, features = msa_ref.shape
    hidden = left_ref.shape[0]
    width = hidden * seqs
    chips, part, _ = second.shape
    left_rows = first.shape[1] - part
    pairs = width // hidden
    spread = ones_where(iota((hidden, width), 1) // seqs == iota((hidden, width), 0))
    right_copies = lax.dot_general(
        right_ref[...], spread, (((0,), (0,)), ((), ())), preferred_element_type=jnp.float32
    )
    right_lane = iota(right_copies.shape, 1) % seqs
    tiled = ones_where(iota((hidden, width), 1) % hidden == iota((hidden, width), 0))
    left_copies = lax.dot_general(
        left_ref[...], tiled, (((0,), (0,)), ((), ())), preferred_element_type=jnp.float32
    ).astype(jnp.bfloat16)
    own_lane = iota((cols, width), 1) // hidden == iota((cols, width), 0) // 2 % pairs
    place = (chips * left_rows, cols)
    target, source = iota(place, 0), iota(place, 1)
    same_pair = (target // left_rows == source // left_rows) & (
        target // seqs % 2 == source % 2
    )
    def replicated(block, send_ref, k):
        return [
            pltpu.make_async_copy(
                block, send_ref.at[pl.ds(group * chips, chips)], sems.at[k, group]
            )
            for group in range(send_ref.shape[0] // chips)
        ]

    right = jnp.zeros((cols, width), jnp.float32)
    normed = []
    for s in range(seqs):
        normed.append(
            standardize_features(msa_ref[s].astype(jnp.float32), gain_ref[...]).astype(
                jnp.bfloat16
            )
        )
        right = right + jnp.dot(
            normed[s],
            jnp.where(right_lane == s, right_copies, 0.0).astype(jnp.bfloat16),
            preferred_element_type=jnp.float32,
        )
    right = right.astype(jnp.bfloat16)
    for chip in range(chips):
        second[chip] = right[part:]
    second_copies = replicated(second, second_ref, 1)
    for copy in second_copies:
        copy.start()
    left = jnp.zeros((chips * left_rows, width), jnp.float32)
    for s in range(seqs):
        products = jnp.dot(normed[s], left_copies, preferred_element_type=jnp.float32)
        left = left + jnp.dot(
            ones_where(same_pair & (target % seqs == s)),
            jnp.where(own_lane, products, 0.0).astype(jnp.bfloat16),
            preferred_element_type=jnp.float32,
        )
    left = left.astype(jnp.bfloat16)
    for chip in range(chips):
        first[chip, :part, :] = right[:part]
        first[chip, part:, :] = left[chip * left_rows : (chip + 1) * left_rows]
    first_copies = replicated(first, first_ref, 0)
    for copy in first_copies:
        copy.start()
    for copy in second_copies + first_copies:
        copy.wait()


def whole(shape):
    return pl.BlockSpec(shape, lambda *_: (0,) * len(shape))


def msa_payload(msa, gain, left, right, groups, chips, left_rows):
    seqs, cols, features = msa.shape
    width = seqs * left.shape[1]
    operands = (msa, gain.reshape(1, features), left.T, right.T)
    return pl.pallas_call(
        msa_kernel,
        grid=(1,),
        in_specs=[whole(operand.shape) for operand in operands],
        out_specs=[pl.BlockSpec(memory_space=pl.ANY)] * 2,
        out_shape=[
            jax.ShapeDtypeStruct((groups * chips, count, width), jnp.bfloat16)
            for count in (cols // 2 + left_rows, cols // 2)
        ],
        scratch_shapes=[
            pltpu.VMEM((chips, cols // 2 + left_rows, width), jnp.bfloat16),
            pltpu.VMEM((chips, cols // 2, width), jnp.bfloat16),
            pltpu.SemaphoreType.DMA((2, groups)),
        ],
        compiler_params=pltpu.CompilerParams(vmem_limit_bytes=58 * MIB),
    )(*operands)


def opm_kernel(
    own, place_ref, gathered_ref, left_ref, weight_ref, out_ref, right_rows, left_block, left_rows, mixer, sems
):
    groups, cols, _ = right_rows.shape
    _, chips, _, width = gathered_ref.shape
    pairs, stacked, hidden = left_rows.shape
    seqs = width // hidden
    channels = weight_ref.shape[1] // hidden
    here = out_ref.shape[0] // 2
    copies = [
        pltpu.make_async_copy(
            gathered_ref.at[:, chip, pl.ds(0, cols), :],
            right_rows.at[:, :, pl.ds(chip * width, width)],
            sems.at[chip],
        )
        for chip in range(chips)
    ]
    left_copy = pltpu.make_async_copy(
        left_ref.at[place_ref[0], :, pl.ds(left_ref.shape[2] - 2 * seqs, 2 * seqs), :],
        left_block,
        sems.at[chips],
    )

    @pl.when(pl.program_id(0) == 0)
    def _():
        left_copy.start()
        for copy in copies:
            copy.start()
        left_copy.wait()
        half = place_ref[1] if own else 1 - place_ref[1]
        half = pl.multiple_of(half * (pairs * hidden), pairs * hidden)
        left = left_block[:, :, pl.ds(half, pairs * hidden)].reshape(stacked, pairs * hidden)
        for pair in range(pairs):
            left_rows[pair] = left[:, pair * hidden : (pair + 1) * hidden]

    step = 16 // seqs
    for pair in range(here):
        expanded = jnp.dot(
            left_rows[pl.program_id(0) * here + pair],
            weight_ref[...],
            preferred_element_type=jnp.float32,
        )
        for chip in range(chips):
            for row in range(2):
                start = (chip * 2 + row) * seqs
                column = (pair * 2 + row) * channels
                for d in range(0, hidden, step):
                    tile = jnp.concatenate(
                        [
                            expanded[start : start + seqs, k * channels : (k + 1) * channels]
                            for k in range(d, d + step)
                        ],
                        axis=0,
                    )
                    mixer[
                        chip * width + d * seqs : chip * width + (d + step) * seqs,
                        column : column + channels,
                    ] = tile.astype(jnp.bfloat16)

    @pl.when(pl.program_id(0) == 0)
    def _():
        for copy in copies:
            copy.wait()

    out = jnp.dot(
        right_rows[...].reshape(groups * cols, chips * width),
        mixer[...],
        preferred_element_type=jnp.float32,
    )
    for row in range(out_ref.shape[0]):
        out_ref[row] = out[:, row * channels : (row + 1) * channels].astype(out_ref.dtype)


def opm_rows(own, place, gathered, left, weight, cols, rows, step_rows=4):
    groups, chips, rows_sent, width = gathered.shape
    hidden = weight.shape[0]
    channels = weight.shape[1] // hidden
    seqs = width // hidden
    return pl.pallas_call(
        functools.partial(opm_kernel, own),
        grid=(rows // step_rows,),
        in_specs=[
            pl.BlockSpec(memory_space=pltpu.SMEM),
            pl.BlockSpec(memory_space=pl.ANY),
            pl.BlockSpec(memory_space=pl.ANY),
            whole(weight.shape),
        ],
        out_specs=pl.BlockSpec((step_rows, groups * cols, channels), lambda i: (i, 0, 0)),
        out_shape=jax.ShapeDtypeStruct((rows, groups * cols, channels), jnp.bfloat16),
        scratch_shapes=[
            pltpu.VMEM((groups, cols, chips * width), jnp.bfloat16),
            pltpu.VMEM((chips, 2 * seqs, width), jnp.bfloat16),
            pltpu.VMEM((rows // 2, chips * 2 * seqs, hidden), jnp.bfloat16),
            pltpu.VMEM((chips * width, step_rows * channels), jnp.bfloat16),
            pltpu.SemaphoreType.DMA((chips + 1,)),
        ],
        compiler_params=pltpu.CompilerParams(vmem_limit_bytes=24 * MIB),
        cost_estimate=pl.CostEstimate(
            flops=2 * rows * groups * cols * chips * width * channels,
            bytes_accessed=gathered.size * 2 + rows * groups * cols * channels * 2,
            transcendentals=0,
        ),
    )(place, gathered, left, weight)


def half_sigmoid(values):
    return 0.5 * jnp.tanh(0.5 * values) + 0.5


def pair_kernel(
    scale, pair_ref, own_ref, arrived_ref, gain_ref, *rest
):
    *weight_refs, updated_ref, normed_ref, send_ref, rows_buf, weight_buf = rest
    rows, cols, width = own_ref.shape
    channels = weight_refs[0].shape[1]

    @pl.when(pl.program_id(0) == 0)
    def _():
        for k, weight_ref in enumerate(weight_refs):
            weight_buf[k * channels : (k + 1) * channels, :] = weight_ref[...].T

    for row in range(rows):
        updated = (
            pair_ref[row].reshape(cols, width).astype(jnp.float32)
            + (own_ref[row].astype(jnp.float32) + arrived_ref[row].astype(jnp.float32)) * scale
        ).astype(jnp.bfloat16)
        updated_ref[row] = updated
        normed = standardize_features(updated.astype(jnp.float32), gain_ref[...]).astype(
            jnp.bfloat16
        )
        normed_ref[row] = normed
        products = lax.dot_general(
            weight_buf[...], normed, (((1,), (1,)), ((), ())), preferred_element_type=jnp.float32
        )
        for side in range(2):
            start = 2 * side * channels
            gated = products[start : start + channels] * half_sigmoid(
                products[start + channels : start + 2 * channels]
            )
            for lane in range(0, cols, 128):
                rows_buf[lane // 128, pl.ds(side * rows + row, channels, stride=2 * rows), :] = (
                    gated[:, lane : lane + 128]
                )
    for lane in range(0, cols, 128):
        send_ref[:, :, lane : lane + 128] = (
            rows_buf[lane // 128, : channels * 2 * rows, :]
            .reshape(channels, 2 * rows, 128)
            .astype(jnp.bfloat16)
        )


def pair_operands(half, pair, own, arrived, gain, weights, scale):
    rows, length, width = own.shape
    groups = pair.shape[1]
    part = length // groups
    channels = weights[0].shape[1]
    cols = 256
    block = pl.BlockSpec((rows, cols, width), lambda i: (0, i, 0))
    return pl.pallas_call(
        functools.partial(pair_kernel, scale),
        grid=(length // cols,),
        in_specs=[
            pl.BlockSpec((rows, cols // part, part, width), lambda i: (0, i, half, 0)),
            block,
            block,
            pl.BlockSpec((1, width), lambda i: (0, 0)),
        ]
        + [whole(weight.shape) for weight in weights],
        out_specs=[
            block,
            block,
            pl.BlockSpec((channels, 2 * rows, cols), lambda i: (0, 0, i)),
        ],
        out_shape=[
            jax.ShapeDtypeStruct(own.shape, jnp.bfloat16),
            jax.ShapeDtypeStruct(own.shape, jnp.bfloat16),
            jax.ShapeDtypeStruct((channels, 2 * rows, length), jnp.bfloat16),
        ],
        scratch_shapes=[
            pltpu.VMEM((cols // 128, (channels + 1) * 2 * rows, 128), jnp.float32),
            pltpu.VMEM((len(weights) * channels, width), jnp.bfloat16),
        ],
        compiler_params=pltpu.CompilerParams(vmem_limit_bytes=18 * MIB),
        cost_estimate=pl.CostEstimate(
            flops=8 * rows * length * width * channels,
            bytes_accessed=rows * length * width * 18,
            transcendentals=2 * rows * length * channels,
        ),
    )(pair, own, arrived, gain.reshape(1, width), *weights)


def result_kernel(mixed_ref, *refs):
    *halves, gain_ref, weight_ref, out_ref, rows_buf = refs
    channels, rows, cols = mixed_ref.shape
    for lane in range(0, cols, 128):
        values = mixed_ref[:, :, lane : lane + 128].astype(jnp.float32)
        center = values - jnp.mean(values, axis=0, keepdims=True)
        spread = jnp.mean(center * center, axis=0, keepdims=True)
        scaled = center * (1.0 / jnp.sqrt(spread + 1e-05))
        rows_buf[: channels * rows, :] = scaled.reshape(channels * rows, 128)
        normed = jnp.concatenate(
            [rows_buf[pl.ds(row, channels, stride=rows), :] * gain_ref[...] for row in range(rows)],
            axis=1,
        ).astype(jnp.bfloat16)
        term = lax.dot_general(
            normed, weight_ref[...], (((0,), (0,)), ((), ())), preferred_element_type=jnp.float32
        ).reshape(rows, 128, -1)
        for half in range(2):
            updated_ref, gate_ref = halves[2 * half : 2 * half + 2]
            place = pl.ds(lane // 2, 64)
            out_ref[:, lane + 64 * half : lane + 64 * half + 64, :] = (
                updated_ref[:, place, :].astype(jnp.float32)
                + gate_ref[:, place, :].astype(jnp.float32)
                * term[:, 64 * half : 64 * half + 64]
            ).astype(jnp.bfloat16)


def result_rows(mixed, halves, gain, weight):
    channels, rows, length = mixed.shape
    width = weight.shape[1]
    cols = 256
    half_block = pl.BlockSpec((rows, cols // 2, width), lambda i: (0, i, 0))
    return pl.pallas_call(
        result_kernel,
        grid=(length // cols,),
        in_specs=[pl.BlockSpec((channels, rows, cols), lambda i: (0, 0, i))]
        + [half_block] * len(halves)
        + [whole((channels, 1)), whole(weight.shape)],
        out_specs=pl.BlockSpec((rows, cols, width), lambda i: (0, i, 0)),
        out_shape=jax.ShapeDtypeStruct((rows, length, width), jnp.bfloat16),
        scratch_shapes=[pltpu.VMEM(((channels + 1) * rows, 128), jnp.float32)],
        compiler_params=pltpu.CompilerParams(vmem_limit_bytes=52 * MIB),
        cost_estimate=pl.CostEstimate(
            flops=2 * rows * length * width * channels,
            bytes_accessed=rows * length * width * 8,
            transcendentals=0,
        ),
    )(mixed, *halves, gain.reshape(channels, 1), weight)


def body(
    stacked_relatives_tensor,
    couple_embedding,
    relatives_rescaler,
    averaged_lhs_weights,
    averaged_rhs_weights,
    mean_final_linear,
    couple_scale_vector,
    first_linear_map,
    first_sigmoid_factor,
    second_linear_map,
    second_sigmoid_factor,
    final_sigmoid_factor,
    trio_scale_vector,
    trio_final_linear,
):
    groups, chips, cores = (lax.axis_size(name) for name in ALL)
    devices = groups * chips * cores
    seqs, cols, features = stacked_relatives_tensor.shape
    hidden = averaged_lhs_weights.shape[1]
    depth = seqs * chips * cores
    rows, length, pair_width = couple_embedding.shape

    payloads = msa_payload(
        stacked_relatives_tensor,
        relatives_rescaler,
        averaged_lhs_weights,
        averaged_rhs_weights,
        groups,
        chips,
        cores * rows,
    )
    part = cols // 2
    gathered = [
        lax.all_to_all(
            payload, ("dap", "chip"), split_axis=0, concat_axis=0, tiled=True
        ).reshape(groups, chips, *payload.shape[1:])
        for payload in payloads
    ]
    weight = mean_final_linear.reshape(hidden, hidden * pair_width)
    place = jnp.stack([lax.axis_index("dap"), lax.axis_index("core")])
    pair = couple_embedding.reshape(rows, groups, cols, pair_width)
    tri_weights = (
        first_linear_map, first_sigmoid_factor, second_linear_map, second_sigmoid_factor
    )
    halves, operands = [], []
    for half in range(2):
        other_part = opm_rows(False, place, gathered[half], gathered[0], weight, part, rows)
        arrived = lax.ppermute(other_part, "core", [(0, 1), (1, 0)])
        own_part = opm_rows(True, place, gathered[half], gathered[0], weight, part, rows)
        updated, pair_normed, send = pair_operands(
            half, pair, own_part, arrived, couple_scale_vector, tri_weights, 1.0 / depth
        )
        gate = jax.nn.sigmoid(
            jnp.dot(pair_normed, final_sigmoid_factor, preferred_element_type=jnp.float32)
        ).astype(jnp.bfloat16)
        halves += [updated, gate]
        operands.append(lax.all_to_all(send, ALL, split_axis=0, concat_axis=0, tiled=True))
    products = [
        functools.partial(
            lax.dot_general,
            operand[:, :rows].reshape(devices * rows, length // 2),
            operand[:, rows:].reshape(devices * rows, length // 2),
            (((1,), (1,)), ((), ())),
            preferred_element_type=jnp.float32,
        )
        for operand in operands
    ]
    first_half = lax.optimization_barrier(products[0]().astype(jnp.bfloat16))
    mixed = (first_half.astype(jnp.float32) + products[1]()).astype(jnp.bfloat16)
    mixed_back = lax.all_to_all(
        mixed.reshape(devices, rows, length), ALL, split_axis=0, concat_axis=0, tiled=True
    )
    return result_rows(mixed_back, halves, trio_scale_vector, trio_final_linear)


def solution(mesh):
    groups, lanes = mesh.shape["dap"], mesh.shape["bulk"]
    fine = Mesh(mesh.devices.reshape(groups, lanes // 2, 2), ALL)
    return jax.shard_map(
        body,
        mesh=fine,
        in_specs=(P(("chip", "core"), "dap", None), P(ALL, None, None)) + (P(),) * 12,
        out_specs=P(ALL, None, None),
        check_vma=False,
    )
```
